128 devices in a mesh: wide: 64 (over x, z, y_lo, core), narrow: 2 (over y_hi).
Axes of the slice: x: 4, y: 4 (y_hi: 2, y_lo: 2; y = y_hi * 2 + y_lo), z: 4, core: 2. Of those that a mesh axis runs over, the one named last changes fastest.
Arguments:
- dosage: bfloat16 [2048, 131072], P(None, 'wide'), may hold values from -4 to 6, as said below
- annotations: int32 [128, 131072], P(None, 'wide'), may hold values from 0 to 1, as said below
- test_statistic_table: float32 [131072, 512], P('wide', 'narrow'), may hold values from 0 to 200
Outputs:
- ld_scores: float32 [128, 131072], P(None, ('wide', 'narrow'))
- fitted: float32 [131072, 512], P('wide', 'narrow')
The draws below stay inside these ranges and needn't reach their ends.
Inputs may be any that keep to these rules, and one draw needn't show every extreme that they name: `dosage`: dosages of each variant follow a correlated process along the variants. `annotations`: 1 where a variant belongs to an annotation.
All inputs are finite; a program needn't handle non-finite values.
Results may differ from the reference program's by a relative error of at most 0.0023.
Values may be sent and summed in bfloat16 or wider, within the bound.
A program may use at most 128 MiB of HBM per device.

```python
import jax
import jax.numpy as jnp
from jax import lax

SAMPLES = 2048
HALF = 1024
ANNOT = 128
TRAITS = 512
LOCUS_COUNT = 131072


def shared_rates(key):
    ambient_seed, maximum_seed, elevated_random_stream = jax.random.split(jax.random.fold_in(key, 101), 3)
    typical_exchange_intensity = jnp.exp(jax.random.uniform(ambient_seed, (LOCUS_COUNT,), minval=jnp.log(0.1 / HALF), maxval=jnp.log(3.0 / HALF)))
    exchange_ceiling = jax.random.uniform(maximum_seed, (LOCUS_COUNT,)) < 4.0 / HALF
    elevated_exchange_profile = jax.random.uniform(elevated_random_stream, (LOCUS_COUNT,), minval=0.2, maxval=0.7)
    return typical_exchange_intensity + jnp.where(exchange_ceiling, elevated_exchange_profile, 0.0)


def shared_annotations(key):
    ambient_seed, key_mult, key_member = jax.random.split(jax.random.fold_in(key, 202), 3)
    base_level = jax.random.randint(ambient_seed, (ANNOT, 1), 40, 200)
    multiplier = jax.random.randint(key_mult, (ANNOT, LOCUS_COUNT // (2 * HALF)), 1, 4)
    thresh = jnp.repeat(multiplier, 2 * HALF, axis=1) * base_level
    uniform_draw = jax.random.randint(key_member, (ANNOT, LOCUS_COUNT), 0, 1024)
    return (uniform_draw < thresh).astype(jnp.int32)


def draw_annotations(key, part):
    return shared_annotations(key)


def draw_dosage(key, part):
    persist = jnp.exp(-shared_rates(key))
    keys = jax.random.split(jax.random.fold_in(key, 303), 6)
    fresh_noise_term = jax.random.normal(keys[0], (LOCUS_COUNT, SAMPLES))
    initial = jax.random.normal(keys[1], (SAMPLES,))

    def advance(state_now, inputs):
        factor, fresh = inputs
        following = factor * state_now + jnp.sqrt(1.0 - factor * factor) * fresh
        return (following, following)
    unused, latent = lax.scan(advance, initial, (persist, fresh_noise_term))
    latent = jnp.clip(latent, -5.0, 5.0)
    offset = jax.random.uniform(keys[4], (LOCUS_COUNT,), minval=0.2, maxval=1.8)
    scales = jnp.exp(jax.random.uniform(keys[5], (LOCUS_COUNT,), minval=jnp.log(0.2), maxval=jnp.log(0.6)))
    values = jnp.clip(offset[:, None] + scales[:, None] * latent, -4.0, 6.0)
    return values.T.astype(jnp.bfloat16)


def draw_test_statistic_table(key, part):
    decay = jnp.exp(-2.0 * shared_rates(key))
    member = shared_annotations(key).astype(jnp.float32).T
    member = member - jnp.mean(member, axis=0)[None, :]

    def carry_on(state_now, inputs):
        factor, fresh = inputs
        following = factor * state_now + fresh
        return (following, following)
    zeros_row = jnp.zeros((ANNOT,), jnp.float32)
    unused, forward = lax.scan(carry_on, zeros_row, (decay, member))
    next_decay = jnp.concatenate([decay[1:], jnp.zeros((1,), jnp.float32)])
    unused_back, backward = lax.scan(carry_on, zeros_row, (next_decay, member), reverse=True)
    proxy = forward + backward - member
    proxy = proxy / (jnp.std(proxy, axis=0)[None, :] + 0.001)
    keys = jax.random.split(jax.random.fold_in(key, 404), 6)
    effects = jax.random.normal(keys[0], (ANNOT, TRAITS)) / jnp.sqrt(float(ANNOT))
    signal = jnp.tanh(jnp.dot(proxy, effects, precision=lax.Precision.HIGHEST))
    position = jnp.arange(LOCUS_COUNT, dtype=jnp.float32) / LOCUS_COUNT
    row_scale = (1.0 + 2.0 * position) / 3.0 * jnp.exp(jax.random.uniform(keys[1], (LOCUS_COUNT,), minval=0.0, maxval=jnp.log(10.0)))
    col_scale = jnp.exp(jax.random.uniform(keys[2], (TRAITS,), minval=jnp.log(0.3), maxval=jnp.log(3.0)))
    gauss = jnp.clip(jax.random.normal(keys[5], (LOCUS_COUNT, TRAITS)), -4.0, 4.0)
    baseline = 0.3 + gauss * gauss
    values = row_scale[:, None] * col_scale[None, :] * baseline * (1.0 + 0.6 * signal) / 4.0
    return jnp.clip(values, 0.0, 200.0).astype(jnp.float32)


def setup_inputs(seed: int = 0) -> dict:
    key_of = jax.random.split(jax.random.key(seed), 4)
    dosage = draw_dosage(jax.random.fold_in(key_of[3], 71), 0)
    annotations = draw_annotations(jax.random.fold_in(key_of[3], 71), 0)
    test_statistic_table = draw_test_statistic_table(jax.random.fold_in(key_of[3], 71), 0)
    return {"dosage": dosage, "annotations": annotations, "test_statistic_table": test_statistic_table}


highest_precision = lax.Precision.HIGHEST

def band_weights(col_geno, row_geno, col_start, row_start, total_variants):
    products = lax.dot_general(col_geno.astype(jnp.float32), row_geno.astype(jnp.float32), (((0,), (0,)), ((), ())), preferred_element_type=jnp.float32)
    samples = row_geno.shape[0]
    correlation = products / samples
    squared = correlation * correlation
    adjusted = squared - (1.0 - squared) / (samples - 2)
    col_index = col_start + jnp.arange(col_geno.shape[1], dtype=jnp.int32)[:, None]
    row_index = row_start + jnp.arange(row_geno.shape[1], dtype=jnp.int32)[None, :]
    inside = (jnp.abs(row_index - col_index) <= HALF) & (col_index >= 0) & (col_index < total_variants)
    return jnp.where(inside, adjusted, 0.0).astype(jnp.bfloat16)

def reference(dosage, annotations, test_statistic_table):
    values = dosage.astype(jnp.float32)
    average = lax.optimization_barrier(jnp.mean(values, axis=0))
    centred_values = values - average[None, :]
    variance = lax.optimization_barrier(jnp.mean(centred_values * centred_values, axis=0))
    standard = (centred_values / jnp.sqrt(variance + 1e-05)[None, :]).astype(jnp.bfloat16)
    shares = lax.optimization_barrier(jnp.sum(annotations.astype(jnp.float32), axis=1)) / LOCUS_COUNT
    centred = (annotations.astype(jnp.float32) - shares[:, None]).astype(jnp.bfloat16)
    padded_geno = jnp.pad(standard, ((0, 0), (HALF, HALF)))
    padded_annot = jnp.pad(centred, ((0, 0), (HALF, HALF)))

    def strip_block(block):
        start = (block * HALF).astype(jnp.int32)
        own_rows = lax.dynamic_slice_in_dim(standard, start, HALF, 1)
        col_geno = lax.dynamic_slice_in_dim(padded_geno, start, 3 * HALF, 1)
        col_annot = lax.dynamic_slice_in_dim(padded_annot, start, 3 * HALF, 1)
        weights = band_weights(col_geno, own_rows, start - HALF, start, LOCUS_COUNT)
        return jnp.dot(col_annot.astype(jnp.float32), weights.astype(jnp.float32), preferred_element_type=jnp.float32)
    blocks = lax.map(strip_block, jnp.arange(LOCUS_COUNT // HALF, dtype=jnp.int32))
    scores = jnp.transpose(blocks, (1, 0, 2)).reshape(ANNOT, LOCUS_COUNT)
    score_mean = lax.optimization_barrier(jnp.sum(scores, axis=1)) / LOCUS_COUNT
    deviation = scores - score_mean[:, None]
    score_var = lax.optimization_barrier(jnp.sum(deviation * deviation, axis=1)) / LOCUS_COUNT
    ld_scores = deviation / jnp.sqrt(score_var + 1e-05)[:, None]
    chi_mean = lax.optimization_barrier(jnp.sum(test_statistic_table, axis=0)) / LOCUS_COUNT
    gram_matrix = jnp.dot(ld_scores.astype(jnp.float32), ld_scores.T.astype(jnp.float32), precision=highest_precision, preferred_element_type=jnp.float32) / LOCUS_COUNT
    projection = jnp.dot(ld_scores.astype(jnp.float32), (test_statistic_table - chi_mean[None, :]).astype(jnp.float32), precision=highest_precision, preferred_element_type=jnp.float32) / LOCUS_COUNT
    coefficient = jnp.linalg.solve(gram_matrix, projection)
    fitted = chi_mean[None, :] + jnp.dot(ld_scores.T.astype(jnp.float32), coefficient.astype(jnp.float32), precision=highest_precision, preferred_element_type=jnp.float32)
    return (ld_scores, fitted)
```

```python
import functools

import jax
import jax.numpy as jnp
from jax import lax
from jax.experimental import pallas as pl
from jax.experimental.pallas import tpu as pltpu
from jax.sharding import PartitionSpec as P

HALF = 1024
MESH = pl.DeviceIdType.MESH


def extended_2(cells, sides, width):
    for axis, dim in sides:
        count = lax.axis_size(axis)
        ends = count - 1
        head = lax.slice_in_dim(cells, 0, width, axis=dim)
        tail = lax.slice_in_dim(cells, cells.shape[dim] - width, cells.shape[dim], axis=dim)
        cells = jnp.concatenate(
            [
                lax.ppermute(tail, axis, [(i, (i + 1) % count) for i in range(ends)]),
                cells,
                lax.ppermute(head, axis, [((i + 1) % count, i) for i in range(ends)]),
            ],
            axis=dim,
        )
    return cells


def band_weights(col_geno, row_geno, col_start, row_start, total_variants):
    products = lax.dot_general(
        col_geno, row_geno, (((0,), (0,)), ((), ())), preferred_element_type=jnp.float32
    )
    samples = row_geno.shape[0]
    correlation = products / samples
    squared = correlation * correlation
    adjusted = squared - (1.0 - squared) / (samples - 2)
    col_index = col_start + jnp.arange(col_geno.shape[1], dtype=jnp.int32)[:, None]
    row_index = row_start + jnp.arange(row_geno.shape[1], dtype=jnp.int32)[None, :]
    inside = (
        (jnp.abs(row_index - col_index) <= HALF) & (col_index >= 0) & (col_index < total_variants)
    )
    return jnp.where(inside, adjusted, 0.0).astype(jnp.bfloat16)


def split(x):
    hi = x.astype(jnp.bfloat16)
    return hi, (x - hi.astype(jnp.float32)).astype(jnp.bfloat16)


def dot3(a, b, dims):
    ah, al = a
    bh, bl = b
    dg = functools.partial(
        lax.dot_general, dimension_numbers=(dims, ((), ())), preferred_element_type=jnp.float32
    )
    return dg(ah, bh) + (dg(ah, bl) + dg(al, bh))


TILES = 64


def stats_kernel(s_ref, t_ref, out_ref, part, got1, sum1, got2, sum2, got3, send, recv):
    w = lax.axis_index("wide")
    g = lax.rem(w, 8)
    h = lax.div(w, 8)

    barrier = pltpu.get_barrier_semaphore()
    for d in range(1, 8):
        pl.semaphore_signal(
            barrier, inc=1, device_id={"wide": w - g + lax.rem(g + d, 8)}, device_id_type=MESH
        )
        pl.semaphore_signal(
            barrier, inc=1, device_id={"wide": lax.rem(h + d, 8) * 8 + g}, device_id_type=MESH
        )

    s = s_ref[...]
    t = t_ref[...]
    ss = split(s)
    ts = split(t)
    part[0:128, :] = dot3(ss, ss, ((1,), (1,)))
    proj = dot3(ss, ts, ((1,), (0,)))
    part[128:256, :] = proj[:, :128]
    part[256:384, :] = proj[:, 128:]
    ones = jnp.ones((8, s.shape[1]), jnp.bfloat16)
    dg = functools.partial(lax.dot_general, preferred_element_type=jnp.float32)
    ssum = dg(ones, ss[0], (((1,), (1,)), ((), ()))) + dg(ones, ss[1], (((1,), (1,)), ((), ())))
    tsum = jnp.sum(t, axis=0, keepdims=True)
    rows = lax.broadcasted_iota(jnp.int32, (8, 128), 0)
    sums = jnp.where(rows == 0, ssum, 0.0)
    sums = jnp.where(rows == 1, tsum[:, :128], sums)
    sums = jnp.where(rows == 2, tsum[:, 128:], sums)
    part[384:392, :] = sums
    part[392:512, :] = jnp.zeros((120, 128), jnp.float32)

    pl.semaphore_wait(barrier, 14)

    def in_block(d):
        return lax.rem(g + d, 8)

    def across(d):
        return lax.rem(h + d, 8)

    def copy1(d):
        p = in_block(d)
        return pltpu.make_async_remote_copy(
            src_ref=part.at[pl.ds(pl.multiple_of(p * 64, 64), 64)],
            dst_ref=got1.at[d - 1],
            send_sem=send.at[0, d],
            recv_sem=recv.at[0, d],
            device_id={"wide": w - g + p},
            device_id_type=MESH,
        )

    def copy2(d):
        p = across(d)
        return pltpu.make_async_remote_copy(
            src_ref=sum1.at[pl.ds(pl.multiple_of(p * 8, 8), 8)],
            dst_ref=got2.at[d - 1],
            send_sem=send.at[1, d],
            recv_sem=recv.at[1, d],
            device_id={"wide": p * 8 + g},
            device_id_type=MESH,
        )

    def copy3(d):
        return pltpu.make_async_remote_copy(
            src_ref=sum2,
            dst_ref=got3.at[pl.ds(pl.multiple_of(h * 8, 8), 8)],
            send_sem=send.at[2, d],
            recv_sem=recv.at[2, d],
            device_id={"wide": across(d) * 8 + g},
            device_id_type=MESH,
        )

    def copy4(d):
        return pltpu.make_async_remote_copy(
            src_ref=got3,
            dst_ref=out_ref.at[pl.ds(pl.multiple_of(g * 64, 64), 64)],
            send_sem=send.at[3, d],
            recv_sem=recv.at[3, d],
            device_id={"wide": w - g + in_block(d)},
            device_id_type=MESH,
        )

    for d in range(1, 8):
        copy1(d).start()
    acc = part[pl.ds(pl.multiple_of(g * 64, 64), 64), :]
    for d in range(1, 8):
        copy1(d).wait_recv()
        acc = acc + got1[d - 1]
    sum1[...] = acc
    for d in range(1, 8):
        copy2(d).start()
    acc = sum1[pl.ds(pl.multiple_of(h * 8, 8), 8), :]
    for d in range(1, 8):
        copy2(d).wait_recv()
        acc = acc + got2[d - 1]
    sum2[...] = acc
    for d in range(1, 8):
        copy3(d).start()
    got3[pl.ds(pl.multiple_of(h * 8, 8), 8), :] = acc
    for d in range(1, 8):
        copy3(d).wait_recv()
    for d in range(1, 8):
        copy4(d).start()
    out_ref[pl.ds(pl.multiple_of(g * 64, 64), 64), :] = got3[...]
    for d in range(1, 8):
        copy4(d).wait_recv()
    for copy in (copy1, copy2, copy3, copy4):
        for d in range(1, 8):
            copy(d).wait_send()


def stats(scores, table):
    f32 = jnp.float32
    return pl.pallas_call(
        stats_kernel,
        out_shape=jax.ShapeDtypeStruct((TILES * 8, 128), f32),
        in_specs=[pl.BlockSpec(memory_space=pltpu.VMEM)] * 2,
        out_specs=pl.BlockSpec(memory_space=pltpu.VMEM),
        scratch_shapes=[
            pltpu.VMEM((TILES * 8, 128), f32),
            pltpu.VMEM((7, 64, 128), f32),
            pltpu.VMEM((64, 128), f32),
            pltpu.VMEM((7, 8, 128), f32),
            pltpu.VMEM((8, 128), f32),
            pltpu.VMEM((64, 128), f32),
            pltpu.SemaphoreType.DMA((4, 8)),
            pltpu.SemaphoreType.DMA((4, 8)),
        ],
        compiler_params=pltpu.CompilerParams(
            collective_id=1, has_side_effects=True, vmem_limit_bytes=32 * 1024 * 1024
        ),
        name="stats",
    )(scores, table)


def finish_kernel(total_variants, p_ref, s_ref, ld_ref, fit_ref):
    n = lax.axis_index("narrow")
    scale = 1.0 / total_variants
    sums = p_ref[384:392, :] * scale
    m_row = sums[0:1, :]
    chi = jnp.concatenate([sums[1:2, :], sums[2:3, :]], axis=1)
    ri = lax.broadcasted_iota(jnp.int32, (128, 128), 0)
    ci = lax.broadcasted_iota(jnp.int32, (128, 128), 1)
    eye = ri == ci
    m_col = jnp.sum(jnp.where(eye, jnp.broadcast_to(m_row, (128, 128)), 0.0), axis=1, keepdims=True)
    cov = p_ref[0:128, :] * scale - m_col * m_row
    proj = jnp.concatenate([p_ref[128:256, :], p_ref[256:384, :]], axis=1) * scale - m_col * chi
    var = jnp.sum(jnp.where(eye, cov, 0.0), axis=1, keepdims=True)
    rstd = 1.0 / jnp.sqrt(var + 1e-05)

    half = ld_ref.shape[1]
    own = s_ref[:, pl.ds(pl.multiple_of(n * half, half), half)]
    ld_ref[...] = (own - m_col) * rstd

    sub = lax.broadcasted_iota(jnp.int32, (8, 1), 0)

    def step(i, carry):
        a, b = carry
        for r in range(8):
            col = a[:, r : r + 1]
            ra = a[r : r + 1, :]
            rb = b[r : r + 1, :]
            inv = 1.0 / a[r : r + 1, r : r + 1]
            ra = ra * inv
            rb = rb * inv
            a2 = a - col * ra
            b2 = b - col * rb
            here = sub == r
            a = jnp.concatenate([jnp.where(here, ra, a2[:8]), a2[8:]], axis=0)
            b = jnp.concatenate([jnp.where(here, rb, b2[:8]), b2[8:]], axis=0)
        a = pltpu.roll(jnp.concatenate([a[8:], a[:8]], axis=0), 120, 1)
        b = jnp.concatenate([b[8:], b[:8]], axis=0)
        return a, b

    _, coef = lax.fori_loop(0, 16, step, (cov, proj))
    cs = split(coef)
    rows = 256
    for k in range(fit_ref.shape[0] // rows):
        dev = (s_ref[:, k * rows : (k + 1) * rows] - m_col).T
        fit_ref[k * rows : (k + 1) * rows, :] = chi + dot3(split(dev), cs, ((1,), (0,)))


def finish(totals, scores, traits, total_variants):
    return pl.pallas_call(
        functools.partial(finish_kernel, total_variants),
        out_shape=(
            jax.ShapeDtypeStruct((128, scores.shape[1] // 2), jnp.float32),
            jax.ShapeDtypeStruct((scores.shape[1], traits), jnp.float32),
        ),
        in_specs=[pl.BlockSpec(memory_space=pltpu.VMEM)] * 2,
        out_specs=(pl.BlockSpec(memory_space=pltpu.VMEM),) * 2,
        compiler_params=pltpu.CompilerParams(vmem_limit_bytes=32 * 1024 * 1024),
        name="finish",
    )(totals, scores)


def shards(dosage, annotations, test_statistic_table):
    samples = dosage.shape[0]
    strip_cols = dosage.shape[1]
    half_width = strip_cols // 2
    total_variants = lax.axis_size("wide") * strip_cols
    wide_index = lax.axis_index("wide")
    narrow_index = lax.axis_index("narrow")
    values = dosage.astype(jnp.float32)
    average = jnp.mean(values, axis=0)
    centred_values = values - average[None, :]
    variance = jnp.mean(centred_values * centred_values, axis=0)
    standard = (centred_values / jnp.sqrt(variance + 1e-05)[None, :]).astype(jnp.bfloat16)
    counts = lax.psum(jnp.sum(annotations.astype(jnp.float32), axis=1), "wide")
    shares = counts / total_variants
    centred = (annotations.astype(jnp.float32) - shares[:, None]).astype(jnp.bfloat16)
    stacked = jnp.concatenate([standard, centred], axis=0)
    row_local = narrow_index * half_width
    strip_start = wide_index * strip_cols
    row_start = strip_start + row_local
    own_rows = lax.dynamic_slice_in_dim(standard, row_local, half_width, 1)
    extended = extended_2(stacked, (("wide", 1),), half_width)
    scores = jnp.zeros((centred.shape[0], half_width), jnp.float32)
    for offset in range(3):
        col_block = lax.dynamic_slice_in_dim(
            extended, row_local + offset * half_width, half_width, 1
        )
        weights = band_weights(
            col_block[:samples],
            own_rows,
            row_start - half_width + offset * half_width,
            row_start,
            total_variants,
        )
        scores = scores + jnp.dot(col_block[samples:], weights, preferred_element_type=jnp.float32)
    strip_scores = lax.all_gather(scores, "narrow", axis=1, tiled=True)
    totals = stats(strip_scores, test_statistic_table)
    return finish(totals, strip_scores, test_statistic_table.shape[1], total_variants)


def solution(mesh):
    in_specs = (P(None, "wide"), P(None, "wide"), P("wide", "narrow"))
    out_specs = (P(None, ("wide", "narrow")), P("wide", "narrow"))
    return jax.shard_map(shards, mesh=mesh, in_specs=in_specs, out_specs=out_specs, check_vma=False)
```

```python
import functools

import jax
import jax.numpy as jnp
from jax import lax
from jax.experimental import pallas as pl
from jax.experimental.pallas import tpu as pltpu
from jax.sharding import PartitionSpec as P

MESH = pl.DeviceIdType.MESH


def split(x):
    hi = x.astype(jnp.bfloat16)
    return hi, (x - hi.astype(jnp.float32)).astype(jnp.bfloat16)


def dot3(a, b, dims):
    ah, al = a
    bh, bl = b
    dg = functools.partial(
        lax.dot_general, dimension_numbers=(dims, ((), ())), preferred_element_type=jnp.float32
    )
    return dg(ah, bh) + (dg(ah, bl) + dg(al, bh))


CH = 256
ROWS = 144
FAR = 4096.0


def scores_kernel(
    total_variants, x_ref, ann_ref, out_ref,
    geno, genot, annot, acc, wbuf, cnt, cnt_got, twin_out, twin_got, halo_out, halo_got,
    load_sem, send, recv, csend, crecv,
):
    f32 = jnp.float32
    bf16 = jnp.bfloat16
    w = lax.axis_index("wide")
    n = lax.axis_index("narrow")
    wides = lax.axis_size("wide")
    samples = x_ref.shape[0]
    core = lax.rem(w, 2)
    chip = lax.div(w, 2)
    g = lax.rem(w, 8)
    h = lax.div(w, 8)
    groups = wides // 8
    mate = w + 1 - 2 * core
    over = lax.rem(w + 2 * core - 1 + wides, wides)
    left_chip = lax.rem(chip + core - 1 + wides // 2, wides // 2)
    turned = lax.rem(left_chip, 2)
    p = n + turned - 2 * n * turned
    ob = core * 4
    mb = 4 - ob
    csl = 2 * core + p

    def device(wide, narrow):
        return {"wide": wide, "narrow": narrow}

    def chunk_of(t):
        rest = ob + lax.rem(csl + t + 4, 4)
        return jnp.where(t == 0, ob + csl, jnp.where(t <= 4, mb + t - 1, rest))

    def load(t):
        c = chunk_of(jnp.int32(t))
        return pltpu.make_async_copy(
            x_ref.at[:, pl.ds(pl.multiple_of(c * CH, CH), CH)], geno.at[c], load_sem.at[t]
        )

    for t in range(8):
        load(t).start()

    barrier = pltpu.get_barrier_semaphore()

    def hello(wide, narrow):
        pl.semaphore_signal(barrier, inc=1, device_id=device(wide, narrow), device_id_type=MESH)

    for d in range(1, 8):
        hello(w - g + lax.rem(g + d, 8), n)
    for d in range(1, groups):
        hello(lax.rem(h + d, groups) * 8 + g, n)
    hello(w, 1 - n)
    hello(over, 0)
    hello(over, 1)

    tail = jnp.where(lax.broadcasted_iota(jnp.int32, (16, CH), 0) == 0, 1.0, 0.0).astype(bf16)
    count = jnp.zeros((8, 128), f32)
    for c in range(8):
        a = ann_ref[:, c * CH : (c + 1) * CH].astype(f32).astype(bf16)
        annot[c, 0:128, :] = a
        annot[c, 128:144, :] = tail
        count = count + lax.dot_general(
            jnp.ones((8, CH), bf16), a, (((1,), (1,)), ((), ())), preferred_element_type=f32
        )
    cnt[0] = count
    acc[...] = jnp.zeros_like(acc)
    pl.semaphore_wait(barrier, 7 + groups - 1 + 3)

    def remote(src, dst, s, r, wide, narrow):
        return pltpu.make_async_remote_copy(
            src_ref=src, dst_ref=dst, send_sem=s, recv_sem=r,
            device_id=device(wide, narrow), device_id_type=MESH,
        )

    def count1(d):
        return remote(
            cnt.at[0], cnt_got.at[0, d], csend.at[0, d], crecv.at[0, d],
            w - g + lax.rem(g + d, 8), n,
        )

    def count2(d):
        return remote(
            cnt.at[1], cnt_got.at[1, d], csend.at[1, d], crecv.at[1, d],
            lax.rem(h + d, groups) * 8 + g, n,
        )

    for d in range(1, 8):
        count1(d).start()

    eps = 1e-05

    def standardize(c):
        def total(i, s):
            x = geno[c, pl.ds(pl.multiple_of(i * 128, 128), 128), :].astype(f32)
            return s + jnp.sum(x.reshape(16, 8, CH), axis=0)

        def spread(i, s):
            x = geno[c, pl.ds(pl.multiple_of(i * 128, 128), 128), :].astype(f32) - mean
            return s + jnp.sum((x * x).reshape(16, 8, CH), axis=0)

        zero = jnp.zeros((8, CH), f32)
        blocks = samples // 128
        mean = jnp.sum(lax.fori_loop(0, blocks, total, zero), axis=0, keepdims=True) / samples
        var = jnp.sum(lax.fori_loop(0, blocks, spread, zero), axis=0, keepdims=True) / samples
        inv = 1.0 / jnp.sqrt(var + eps)

        def put(i, _):
            at = pl.ds(pl.multiple_of(i * 128, 128), 128)
            y = ((geno[c, at, :].astype(f32) - mean) * inv).astype(bf16)
            geno[c, at, :] = y
            genot[c, :, at] = y.T
            return 0

        lax.fori_loop(0, blocks, put, 0)

    def halo_geno():
        return remote(
            geno.at[ob + csl], geno.at[12], send.at[0], recv.at[0], over, p
        )

    def halo_annot():
        return remote(
            annot.at[ob + csl], annot.at[12], send.at[1], recv.at[1], over, p
        )

    def mate_geno(q):
        return remote(
            geno.at[mb + q], geno.at[8 + q], send.at[2 + q], recv.at[2 + q], mate, n
        )

    def mate_annot():
        return remote(
            annot.at[pl.ds(mb, 4)], annot.at[pl.ds(8, 4)], send.at[6], recv.at[6], mate, n
        )

    halo_annot().start()
    mate_annot().start()
    load(0).wait()
    standardize(ob + csl)
    halo_geno().start()
    for q in range(4):
        load(1 + q).wait()

    def mate_step(q, _):
        standardize(mb + q)
        mate_geno(q).start()
        return 0

    lax.fori_loop(0, 4, mate_step, 0)
    for t in range(5, 8):
        load(t).wait()

    def rest_step(t, _):
        standardize(ob + lax.rem(csl + t, 4))
        return 0

    lax.fori_loop(1, 4, rest_step, 0)

    total_count = cnt[0]
    for d in range(1, 8):
        count1(d).wait_recv()
        total_count = total_count + cnt_got[0, d]
    cnt[1] = total_count
    for d in range(1, groups):
        count2(d).start()

    k1 = (1.0 + 1.0 / (samples - 2)) / (float(samples) * samples)
    k2 = 1.0 / (samples - 2)
    diff = (
        lax.broadcasted_iota(jnp.int32, (CH, CH), 0) - lax.broadcasted_iota(jnp.int32, (CH, CH), 1)
    ).astype(f32)

    def run(tiles, tile):
        def weigh(t):
            own, other, _, sign, limit, factor = tile(t)
            products = jnp.dot(genot[own], geno[other], preferred_element_type=f32)
            value = (products * products) * (k1 * factor) - k2 * factor
            wbuf[lax.rem(t, 2)] = jnp.where(diff * sign <= limit, value, 0.0).astype(bf16)

        def apply(t):
            own, other, own_sum, _, _, _ = tile(t)
            weights = wbuf[lax.rem(t, 2)]
            acc[other] += jnp.dot(annot[own], weights, preferred_element_type=f32)
            acc[own_sum] += lax.dot_general(
                annot[other], weights, (((1,), (1,)), ((), ())), preferred_element_type=f32
            )

        weigh(jnp.int32(0))

        def step(t, _):
            apply(t - 1)
            weigh(t)
            return 0

        lax.fori_loop(1, tiles, step, 0)
        apply(jnp.int32(tiles - 1))

    def at_least(t, bound):
        return (t >= bound).astype(jnp.int32)

    def local_tile(t):
        off = at_least(t, 8) + at_least(t, 15) + at_least(t, 21) + at_least(t, 26)
        base = 8 * at_least(t, 8) + 7 * at_least(t, 15) + 6 * at_least(t, 21) + 5 * at_least(t, 26)
        low = t - base
        high = low + off
        return (
            high, low, high, 1.0,
            jnp.where(off == 4, 0.0, FAR), jnp.where(off == 0, 0.5, 1.0),
        )

    run(30, local_tile)

    total_count = cnt[1]
    for d in range(1, groups):
        count2(d).wait_recv()
        total_count = total_count + cnt_got[1, d]

    mate_annot().wait_recv()
    for q in range(4):
        mate_geno(q).wait_recv()

    def mate_tile(t):
        u = at_least(t, 1) + at_least(t, 3) + at_least(t, 6)
        v = t - at_least(t, 1) - 2 * at_least(t, 3) - 3 * at_least(t, 6)
        own = mb + jnp.where(core == 0, u, v)
        other = 8 + jnp.where(core == 0, v, u)
        return (
            own, other, own, jnp.where(core == 0, -1.0, 1.0),
            jnp.where(u == v, 0.0, FAR), 1.0,
        )

    run(10, mate_tile)

    halo_annot().wait_recv()
    halo_geno().wait_recv()
    open_end = jnp.where(core == 0, w == 0, w == wides - 1)

    def halo_tile(t):
        far = jnp.where(
            core == 1, 256 * (t - n), jnp.where(t >= 2, 512 + 256 * (n - t), -4096)
        )
        limit = jnp.where(open_end, -4096, far).astype(f32)
        return ob + t, jnp.int32(12), 13 + t, jnp.where(core == 0, 1.0, -1.0), limit, 1.0

    run(4, halo_tile)

    ri = lax.broadcasted_iota(jnp.int32, (128, 128), 0)
    ci = lax.broadcasted_iota(jnp.int32, (128, 128), 1)
    counts = jnp.sum(
        jnp.where(ri == ci, jnp.broadcast_to(total_count[0:1, :], (128, 128)), 0.0),
        axis=1, keepdims=True,
    )
    shares = counts / total_variants
    zero_value = (0.0 - shares).astype(bf16).astype(f32)
    step_value = (1.0 - shares).astype(bf16).astype(f32) - zero_value

    def centred(c):
        return zero_value * acc[c, 128:129, :] + step_value * acc[c, 0:128, :]

    def halo_back(m):
        return remote(
            halo_out, halo_got.at[n], send.at[7 + m], recv.at[7 + n], over, m
        )

    def halo_back_from(m):
        return remote(
            halo_out, halo_got.at[m], send.at[7 + m], recv.at[7 + m], over, m
        )

    def twin(part):
        return remote(
            twin_out.at[pl.ds(2 * part, 2)], twin_got.at[pl.ds(2 * part, 2)],
            send.at[9 + part], recv.at[9 + part], w, 1 - n,
        )

    halo_out[...] = centred(12)
    for m in range(2):
        halo_back(m).start()
    for q in range(4):
        twin_out[q] = centred(13 + q).astype(bf16)
    twin(1).start()

    @pl.when(core == 1)
    def _():
        twin(0).start()

    @pl.when(core == 0)
    def _():
        twin_got[0:2] = jnp.zeros((2, 128, CH), bf16)

    def columns(c):
        return pl.ds(pl.multiple_of(c * CH, CH), CH)

    for q in range(4):
        out_ref[:, columns(mb + q)] = centred(mb + q)
        out_ref[:, columns(ob + q)] = centred(ob + q) + centred(13 + q)
    for m in range(2):
        halo_back_from(m).wait_recv()
        out_ref[:, columns(ob + 2 * core + m)] += halo_got[m]
    twin(1).wait_recv()

    @pl.when(core == 1)
    def _():
        twin(0).wait_recv()

    for q in range(4):
        out_ref[:, columns(ob + q)] += twin_got[q].astype(f32)

    for d in range(1, 8):
        count1(d).wait_send()
    for d in range(1, groups):
        count2(d).wait_send()
    halo_geno().wait_send()
    halo_annot().wait_send()
    mate_annot().wait_send()
    for q in range(4):
        mate_geno(q).wait_send()
    for m in range(2):
        halo_back(m).wait_send()
    twin(1).wait_send()

    @pl.when(core == 1)
    def _():
        twin(0).wait_send()


def strip_scores(dosage, annotations, total_variants):
    f32 = jnp.float32
    bf16 = jnp.bfloat16
    samples = dosage.shape[0]
    dma = pltpu.SemaphoreType.DMA
    return pl.pallas_call(
        functools.partial(scores_kernel, total_variants),
        out_shape=jax.ShapeDtypeStruct((128, 8 * CH), f32),
        in_specs=[pl.BlockSpec(memory_space=pl.ANY), pl.BlockSpec(memory_space=pltpu.VMEM)],
        out_specs=pl.BlockSpec(memory_space=pltpu.VMEM),
        scratch_shapes=[
            pltpu.VMEM((13, samples, CH), bf16),
            pltpu.VMEM((8, CH, samples), bf16),
            pltpu.VMEM((13, ROWS, CH), bf16),
            pltpu.VMEM((17, ROWS, CH), f32),
            pltpu.VMEM((2, CH, CH), bf16),
            pltpu.VMEM((2, 8, 128), f32),
            pltpu.VMEM((2, 8, 8, 128), f32),
            pltpu.VMEM((4, 128, CH), bf16),
            pltpu.VMEM((4, 128, CH), bf16),
            pltpu.VMEM((128, CH), f32),
            pltpu.VMEM((2, 128, CH), f32),
            dma((8,)), dma((11,)), dma((11,)), dma((2, 8)), dma((2, 8)),
        ],
        compiler_params=pltpu.CompilerParams(
            collective_id=0, has_side_effects=True, vmem_limit_bytes=56 * 1024 * 1024
        ),
        name="scores",
    )(dosage, annotations)


TILES = 64


def stats_kernel(s_ref, t_ref, out_ref, part, got1, sum1, got2, sum2, got3, send, recv):
    w = lax.axis_index("wide")
    g = lax.rem(w, 8)
    h = lax.div(w, 8)

    barrier = pltpu.get_barrier_semaphore()
    for d in range(1, 8):
        pl.semaphore_signal(
            barrier, inc=1, device_id={"wide": w - g + lax.rem(g + d, 8)}, device_id_type=MESH
        )
        pl.semaphore_signal(
            barrier, inc=1, device_id={"wide": lax.rem(h + d, 8) * 8 + g}, device_id_type=MESH
        )

    s = s_ref[...]
    t = t_ref[...]
    ss = split(s)
    ts = split(t)
    part[0:128, :] = dot3(ss, ss, ((1,), (1,)))
    proj = dot3(ss, ts, ((1,), (0,)))
    part[128:256, :] = proj[:, :128]
    part[256:384, :] = proj[:, 128:]
    ones = jnp.ones((8, s.shape[1]), jnp.bfloat16)
    dg = functools.partial(lax.dot_general, preferred_element_type=jnp.float32)
    ssum = dg(ones, ss[0], (((1,), (1,)), ((), ()))) + dg(ones, ss[1], (((1,), (1,)), ((), ())))
    tsum = jnp.sum(t, axis=0, keepdims=True)
    rows = lax.broadcasted_iota(jnp.int32, (8, 128), 0)
    sums = jnp.where(rows == 0, ssum, 0.0)
    sums = jnp.where(rows == 1, tsum[:, :128], sums)
    sums = jnp.where(rows == 2, tsum[:, 128:], sums)
    part[384:392, :] = sums
    part[392:512, :] = jnp.zeros((120, 128), jnp.float32)

    pl.semaphore_wait(barrier, 14)

    def in_block(d):
        return lax.rem(g + d, 8)

    def across(d):
        return lax.rem(h + d, 8)

    def copy1(d):
        p = in_block(d)
        return pltpu.make_async_remote_copy(
            src_ref=part.at[pl.ds(pl.multiple_of(p * 64, 64), 64)],
            dst_ref=got1.at[d - 1],
            send_sem=send.at[0, d],
            recv_sem=recv.at[0, d],
            device_id={"wide": w - g + p},
            device_id_type=MESH,
        )

    def copy2(d):
        p = across(d)
        return pltpu.make_async_remote_copy(
            src_ref=sum1.at[pl.ds(pl.multiple_of(p * 8, 8), 8)],
            dst_ref=got2.at[d - 1],
            send_sem=send.at[1, d],
            recv_sem=recv.at[1, d],
            device_id={"wide": p * 8 + g},
            device_id_type=MESH,
        )

    def copy3(d):
        return pltpu.make_async_remote_copy(
            src_ref=sum2,
            dst_ref=got3.at[pl.ds(pl.multiple_of(h * 8, 8), 8)],
            send_sem=send.at[2, d],
            recv_sem=recv.at[2, d],
            device_id={"wide": across(d) * 8 + g},
            device_id_type=MESH,
        )

    def copy4(d):
        return pltpu.make_async_remote_copy(
            src_ref=got3,
            dst_ref=out_ref.at[pl.ds(pl.multiple_of(g * 64, 64), 64)],
            send_sem=send.at[3, d],
            recv_sem=recv.at[3, d],
            device_id={"wide": w - g + in_block(d)},
            device_id_type=MESH,
        )

    for d in range(1, 8):
        copy1(d).start()
    acc = part[pl.ds(pl.multiple_of(g * 64, 64), 64), :]
    for d in range(1, 8):
        copy1(d).wait_recv()
        acc = acc + got1[d - 1]
    sum1[...] = acc
    for d in range(1, 8):
        copy2(d).start()
    acc = sum1[pl.ds(pl.multiple_of(h * 8, 8), 8), :]
    for d in range(1, 8):
        copy2(d).wait_recv()
        acc = acc + got2[d - 1]
    sum2[...] = acc
    for d in range(1, 8):
        copy3(d).start()
    got3[pl.ds(pl.multiple_of(h * 8, 8), 8), :] = acc
    for d in range(1, 8):
        copy3(d).wait_recv()
    for d in range(1, 8):
        copy4(d).start()
    out_ref[pl.ds(pl.multiple_of(g * 64, 64), 64), :] = got3[...]
    for d in range(1, 8):
        copy4(d).wait_recv()
    for copy in (copy1, copy2, copy3, copy4):
        for d in range(1, 8):
            copy(d).wait_send()


def stats(scores, table):
    f32 = jnp.float32
    return pl.pallas_call(
        stats_kernel,
        out_shape=jax.ShapeDtypeStruct((TILES * 8, 128), f32),
        in_specs=[pl.BlockSpec(memory_space=pltpu.VMEM)] * 2,
        out_specs=pl.BlockSpec(memory_space=pltpu.VMEM),
        scratch_shapes=[
            pltpu.VMEM((TILES * 8, 128), f32),
            pltpu.VMEM((7, 64, 128), f32),
            pltpu.VMEM((64, 128), f32),
            pltpu.VMEM((7, 8, 128), f32),
            pltpu.VMEM((8, 128), f32),
            pltpu.VMEM((64, 128), f32),
            pltpu.SemaphoreType.DMA((4, 8)),
            pltpu.SemaphoreType.DMA((4, 8)),
        ],
        compiler_params=pltpu.CompilerParams(
            collective_id=1, has_side_effects=True, vmem_limit_bytes=32 * 1024 * 1024
        ),
        name="stats",
    )(scores, table)


def finish_kernel(total_variants, p_ref, s_ref, ld_ref, fit_ref):
    n = lax.axis_index("narrow")
    scale = 1.0 / total_variants
    sums = p_ref[384:392, :] * scale
    m_row = sums[0:1, :]
    chi = jnp.concatenate([sums[1:2, :], sums[2:3, :]], axis=1)
    ri = lax.broadcasted_iota(jnp.int32, (128, 128), 0)
    ci = lax.broadcasted_iota(jnp.int32, (128, 128), 1)
    eye = ri == ci
    m_col = jnp.sum(jnp.where(eye, jnp.broadcast_to(m_row, (128, 128)), 0.0), axis=1, keepdims=True)
    cov = p_ref[0:128, :] * scale - m_col * m_row
    proj = jnp.concatenate([p_ref[128:256, :], p_ref[256:384, :]], axis=1) * scale - m_col * chi
    var = jnp.sum(jnp.where(eye, cov, 0.0), axis=1, keepdims=True)
    rstd = 1.0 / jnp.sqrt(var + 1e-05)

    half = ld_ref.shape[1]
    own = s_ref[:, pl.ds(pl.multiple_of(n * half, half), half)]
    ld_ref[...] = (own - m_col) * rstd

    sub = lax.broadcasted_iota(jnp.int32, (8, 1), 0)

    def step(i, carry):
        a, b = carry
        for r in range(8):
            col = a[:, r : r + 1]
            ra = a[r : r + 1, :]
            rb = b[r : r + 1, :]
            inv = 1.0 / a[r : r + 1, r : r + 1]
            ra = ra * inv
            rb = rb * inv
            a2 = a - col * ra
            b2 = b - col * rb
            here = sub == r
            a = jnp.concatenate([jnp.where(here, ra, a2[:8]), a2[8:]], axis=0)
            b = jnp.concatenate([jnp.where(here, rb, b2[:8]), b2[8:]], axis=0)
        a = pltpu.roll(jnp.concatenate([a[8:], a[:8]], axis=0), 120, 1)
        b = jnp.concatenate([b[8:], b[:8]], axis=0)
        return a, b

    _, coef = lax.fori_loop(0, 16, step, (cov, proj))
    cs = split(coef)
    rows = 256
    for k in range(fit_ref.shape[0] // rows):
        dev = (s_ref[:, k * rows : (k + 1) * rows] - m_col).T
        fit_ref[k * rows : (k + 1) * rows, :] = chi + dot3(split(dev), cs, ((1,), (0,)))


def finish(totals, scores, traits, total_variants):
    return pl.pallas_call(
        functools.partial(finish_kernel, total_variants),
        out_shape=(
            jax.ShapeDtypeStruct((128, scores.shape[1] // 2), jnp.float32),
            jax.ShapeDtypeStruct((scores.shape[1], traits), jnp.float32),
        ),
        in_specs=[pl.BlockSpec(memory_space=pltpu.VMEM)] * 2,
        out_specs=(pl.BlockSpec(memory_space=pltpu.VMEM),) * 2,
        compiler_params=pltpu.CompilerParams(vmem_limit_bytes=32 * 1024 * 1024),
        name="finish",
    )(totals, scores)


def shards(dosage, annotations, test_statistic_table):
    total_variants = lax.axis_size("wide") * dosage.shape[1]
    scores = strip_scores(dosage, annotations, total_variants)
    totals = stats(scores, test_statistic_table)
    return finish(totals, scores, test_statistic_table.shape[1], total_variants)


def solution(mesh):
    in_specs = (P(None, "wide"), P(None, "wide"), P("wide", "narrow"))
    out_specs = (P(None, ("wide", "narrow")), P("wide", "narrow"))
    return jax.shard_map(shards, mesh=mesh, in_specs=in_specs, out_specs=out_specs, check_vma=False)
```

```python
import functools

import jax
import jax.numpy as jnp
from jax import lax
from jax.experimental import pallas as pl
from jax.experimental.pallas import tpu as pltpu
from jax.sharding import PartitionSpec as P

MESH = pl.DeviceIdType.MESH


def split(x):
    hi = x.astype(jnp.bfloat16)
    return hi, (x - hi.astype(jnp.float32)).astype(jnp.bfloat16)


def dot3(a, b, dims):
    ah, al = a
    bh, bl = b
    dg = functools.partial(
        lax.dot_general, dimension_numbers=(dims, ((), ())), preferred_element_type=jnp.float32
    )
    return dg(ah, bh) + (dg(ah, bl) + dg(al, bh))


CH = 256
ROWS = 144


def scores_kernel(
    total_variants, x_ref, ann_ref, out_ref,
    geno, annot, acc, edge_acc, wbuf, edge, cnt, cnt_got, twin_out, twin_got, halo_out, halo_got,
    load_sem, send, recv, csend, crecv,
):
    f32 = jnp.float32
    bf16 = jnp.bfloat16
    w = lax.axis_index("wide")
    n = lax.axis_index("narrow")
    wides = lax.axis_size("wide")
    samples = x_ref.shape[0]
    core = lax.rem(w, 2)
    chip = lax.div(w, 2)
    g = lax.rem(w, 8)
    h = lax.div(w, 8)
    groups = wides // 8
    mate = w + 1 - 2 * core
    over = lax.rem(w + 2 * core - 1 + wides, wides)
    left_chip = lax.rem(chip + core - 1 + wides // 2, wides // 2)
    turned = lax.rem(left_chip, 2)
    p = n + turned - 2 * n * turned
    csl = 2 * core + p
    base = 4 * core
    outer = 8 * core
    beside = 8 - 8 * core

    def columns(c, count=1):
        return pl.ds(pl.multiple_of(c * CH, CH), count * CH)

    def inner(i):
        return jnp.where(core == 0, 3 - i, i)

    def device(wide, narrow):
        return {"wide": wide, "narrow": narrow}

    def load(t):
        if t == 0:
            c = outer + csl
        elif t <= 4:
            c = 4 + inner(t - 1)
        else:
            c = outer + lax.rem(csl + t - 4, 4)
        return pltpu.make_async_copy(x_ref.at[:, columns(c - base)], geno.at[:, columns(c)], load_sem.at[t])

    for t in range(8):
        load(t).start()

    barrier = pltpu.get_barrier_semaphore()

    def hello(wide, narrow):
        pl.semaphore_signal(barrier, inc=1, device_id=device(wide, narrow), device_id_type=MESH)

    for d in range(1, 8):
        hello(w - g + lax.rem(g + d, 8), n)
    for d in range(1, groups):
        hello(lax.rem(h + d, groups) * 8 + g, n)
    hello(w, 1 - n)
    hello(over, 0)
    hello(over, 1)

    tail = jnp.where(lax.broadcasted_iota(jnp.int32, (16, CH), 0) == 0, 1.0, 0.0).astype(bf16)
    count = jnp.zeros((8, 128), f32)
    for c in range(8):
        a = ann_ref[:, c * CH : (c + 1) * CH].astype(f32).astype(bf16)
        annot[0:128, columns(base + c)] = a
        annot[128:144, columns(base + c)] = tail
        count = count + lax.dot_general(
            jnp.ones((8, CH), bf16), a, (((1,), (1,)), ((), ())), preferred_element_type=f32
        )
    cnt[0] = count
    acc[...] = jnp.zeros_like(acc)
    ri = lax.broadcasted_iota(jnp.int32, (CH, CH), 0)
    ci = lax.broadcasted_iota(jnp.int32, (CH, CH), 1)
    edge[0] = jnp.where(core == 0, 0.5, jnp.where(ci <= ri, 1.0, 0.0))
    edge[1] = jnp.where(core == 1, 0.5, jnp.where(ri <= ci, 1.0, 0.0))
    pl.semaphore_wait(barrier, 7 + groups - 1 + 3)

    def remote(src, dst, s, r, wide, narrow):
        return pltpu.make_async_remote_copy(
            src_ref=src, dst_ref=dst, send_sem=s, recv_sem=r,
            device_id=device(wide, narrow), device_id_type=MESH,
        )

    def count1(d):
        return remote(
            cnt.at[0], cnt_got.at[0, d], csend.at[0, d], crecv.at[0, d],
            w - g + lax.rem(g + d, 8), n,
        )

    def count2(d):
        return remote(
            cnt.at[1], cnt_got.at[1, d], csend.at[1, d], crecv.at[1, d],
            lax.rem(h + d, groups) * 8 + g, n,
        )

    for d in range(1, 8):
        count1(d).start()

    eps = 1e-05

    def standardize(c):
        at = columns(c)
        block = 256

        def rows(i):
            return pl.ds(pl.multiple_of(i * block, block), block)

        pivot = geno[0:16, at].astype(f32)[0:1]

        def sums(i, s):
            x = (geno[rows(i), at].astype(f32) - pivot).reshape(block // 8, 8, CH)
            return s[0] + jnp.sum(x, axis=0), s[1] + jnp.sum(x * x, axis=0)

        zero = jnp.zeros((8, CH), f32)
        first, second = lax.fori_loop(0, samples // block, sums, (zero, zero))
        shift = jnp.sum(first, axis=0, keepdims=True) / samples
        var = jnp.sum(second, axis=0, keepdims=True) / samples - shift * shift
        mean = pivot + shift
        inv = 1.0 / jnp.sqrt(jnp.maximum(var, 0.0) + eps)

        def put(i, _):
            geno[rows(i), at] = ((geno[rows(i), at].astype(f32) - mean) * inv).astype(bf16)
            return 0

        lax.fori_loop(0, samples // block, put, 0)

    def halo_geno():
        return remote(
            geno.at[:, columns(outer + csl)], geno.at[:, columns(12)], send.at[0], recv.at[0], over, p
        )

    def halo_annot():
        return remote(
            annot.at[:, columns(outer + csl)], annot.at[:, columns(12)], send.at[1], recv.at[1], over, p
        )

    def mate_geno(q):
        return remote(
            geno.at[:, columns(4 + q)], geno.at[:, columns(outer + q)],
            send.at[2 + q], recv.at[2 + q], mate, n,
        )

    def mate_geno_from(q):
        return remote(
            geno.at[:, columns(4 + q)], geno.at[:, columns(beside + q)],
            send.at[2 + q], recv.at[2 + q], mate, n,
        )

    def mate_annot():
        return remote(
            annot.at[:, columns(4, 4)], annot.at[:, columns(outer, 4)], send.at[6], recv.at[6], mate, n
        )

    def mate_annot_from():
        return remote(
            annot.at[:, columns(4, 4)], annot.at[:, columns(beside, 4)], send.at[6], recv.at[6], mate, n
        )

    halo_annot().start()
    mate_annot().start()
    load(0).wait()
    standardize(outer + csl)
    halo_geno().start()
    for q in range(4):
        load(1 + q).wait()

    def mate_step(i, _):
        standardize(4 + inner(i))
        mate_geno(inner(i)).start()
        return 0

    lax.fori_loop(0, 4, mate_step, 0)
    for t in range(5, 8):
        load(t).wait()

    def rest_step(t, _):
        standardize(outer + lax.rem(csl + t, 4))
        return 0

    lax.fori_loop(1, 4, rest_step, 0)

    total_count = cnt[0]
    for d in range(1, 8):
        count1(d).wait_recv()
        total_count = total_count + cnt_got[0, d]
    cnt[1] = total_count
    for d in range(1, groups):
        count2(d).start()

    k1 = (1.0 + 1.0 / (samples - 2)) / (float(samples) * samples)
    k2 = 1.0 / (samples - 2)
    diff = (
        lax.broadcasted_iota(jnp.int32, (CH, CH), 0) - lax.broadcasted_iota(jnp.int32, (CH, CH), 1)
    ).astype(f32)

    def correlate(own, other):
        products = lax.dot_general(
            geno[:, columns(own)], geno[:, columns(other)], (((0,), (0,)), ((), ())),
            preferred_element_type=f32,
        )
        return (products * products) * k1 - k2

    def place(t):
        return jnp.where(core == 0, t, 7 - t), jnp.where(core == 0, t, 11 - t)

    def weigh(t):
        own, other = place(t)
        for b in range(5):
            value = correlate(own + b, other)
            if b in (0, 4):
                value = value * edge[b // 4]
            wbuf[lax.rem(t, 2), b * CH : (b + 1) * CH, :] = value.astype(bf16)

    def apply(t):
        own, other = place(t)
        weights = wbuf[lax.rem(t, 2)]
        acc[:, columns(other)] += jnp.dot(
            annot[:, columns(own, 5)], weights, preferred_element_type=f32
        )
        acc[:, columns(own, 5)] += lax.dot_general(
            annot[:, columns(other)], weights, (((1,), (1,)), ((), ())), preferred_element_type=f32
        )

    def step(t, _):
        apply(t - 1)
        weigh(t)
        return 0

    def late_step(t, _):
        mate_geno_from(jnp.where(core == 0, t - 4, 7 - t)).wait_recv()
        return step(t, 0)

    weigh(jnp.int32(0))
    lax.fori_loop(1, 4, step, 0)
    total_count = cnt[1]
    for d in range(1, groups):
        count2(d).wait_recv()
        total_count = total_count + cnt_got[1, d]
    mate_annot_from().wait_recv()
    lax.fori_loop(4, 8, late_step, 0)

    halo_annot().wait_recv()
    halo_geno().wait_recv()
    apply(jnp.int32(7))
    open_end = jnp.where(core == 0, w == 0, w == wides - 1)
    near = jnp.where(open_end, 8192, jnp.where(core == 0, -8192, CH * n))
    far = jnp.where(core == 0, 512 + CH * n, 8192)
    first_row = jnp.where(core == 0, 512, 0)
    for b in range(4):
        row = ri + b * CH
        diff = row - ci
        inside = (diff >= near) & (diff <= far) & (row >= first_row)
        value = jnp.where(inside, correlate(outer + b, 12), 0.0)
        wbuf[0, b * CH : (b + 1) * CH, :] = value.astype(bf16)
    weights = wbuf[0, 0 : 4 * CH, :]
    acc[:, columns(12)] = jnp.dot(
        annot[:, columns(outer, 4)], weights, preferred_element_type=f32
    )
    edge_acc[...] = lax.dot_general(
        annot[:, columns(12)], weights, (((1,), (1,)), ((), ())), preferred_element_type=f32
    )

    eye = ri[:128, :128] == ci[:128, :128]
    counts = jnp.sum(
        jnp.where(eye, jnp.broadcast_to(total_count[0:1, :], (128, 128)), 0.0),
        axis=1, keepdims=True,
    )
    shares = counts / total_variants
    zero_value = (0.0 - shares).astype(bf16).astype(f32)
    step_value = (1.0 - shares).astype(bf16).astype(f32) - zero_value

    def centred(sums):
        return zero_value * sums[128:129, :] + step_value * sums[0:128, :]

    def halo_back(m):
        return remote(
            halo_out, halo_got.at[n], send.at[7 + m], recv.at[7 + n], over, m
        )

    def halo_back_from(m):
        return remote(
            halo_out, halo_got.at[m], send.at[7 + m], recv.at[7 + m], over, m
        )

    def twin(part):
        return remote(
            twin_out.at[pl.ds(2 * part, 2)], twin_got.at[pl.ds(2 * part, 2)],
            send.at[9 + part], recv.at[9 + part], w, 1 - n,
        )

    halo_out[...] = centred(acc[:, columns(12)])
    for m in range(2):
        halo_back(m).start()
    for q in range(4):
        twin_out[q] = centred(edge_acc[:, q * CH : (q + 1) * CH]).astype(bf16)
    twin(1).start()

    @pl.when(core == 1)
    def _():
        twin(0).start()

    @pl.when(core == 0)
    def _():
        twin_got[0:2] = jnp.zeros((2, 128, CH), bf16)

    def out(c):
        return columns(c - base)

    for q in range(4):
        out_ref[:, out(4 + q)] = centred(acc[:, columns(4 + q)])
        out_ref[:, out(outer + q)] = centred(
            acc[:, columns(outer + q)] + edge_acc[:, q * CH : (q + 1) * CH]
        )
    for m in range(2):
        halo_back_from(m).wait_recv()
        out_ref[:, out(outer + 2 * core + m)] += halo_got[m]
    twin(1).wait_recv()

    @pl.when(core == 1)
    def _():
        twin(0).wait_recv()

    for q in range(4):
        out_ref[:, out(outer + q)] += twin_got[q].astype(f32)

    for d in range(1, 8):
        count1(d).wait_send()
    for d in range(1, groups):
        count2(d).wait_send()
    halo_geno().wait_send()
    halo_annot().wait_send()
    mate_annot().wait_send()
    for q in range(4):
        mate_geno(q).wait_send()
    for m in range(2):
        halo_back(m).wait_send()
    twin(1).wait_send()

    @pl.when(core == 1)
    def _():
        twin(0).wait_send()


def strip_scores(dosage, annotations, total_variants):
    f32 = jnp.float32
    bf16 = jnp.bfloat16
    samples = dosage.shape[0]
    dma = pltpu.SemaphoreType.DMA
    return pl.pallas_call(
        functools.partial(scores_kernel, total_variants),
        out_shape=jax.ShapeDtypeStruct((128, 8 * CH), f32),
        in_specs=[pl.BlockSpec(memory_space=pl.ANY), pl.BlockSpec(memory_space=pltpu.VMEM)],
        out_specs=pl.BlockSpec(memory_space=pltpu.VMEM),
        scratch_shapes=[
            pltpu.VMEM((samples, 13 * CH), bf16),
            pltpu.VMEM((ROWS, 13 * CH), bf16),
            pltpu.VMEM((ROWS, 13 * CH), f32),
            pltpu.VMEM((ROWS, 4 * CH), f32),
            pltpu.VMEM((2, 5 * CH, CH), bf16),
            pltpu.VMEM((2, CH, CH), f32),
            pltpu.VMEM((2, 8, 128), f32),
            pltpu.VMEM((2, 8, 8, 128), f32),
            pltpu.VMEM((4, 128, CH), bf16),
            pltpu.VMEM((4, 128, CH), bf16),
            pltpu.VMEM((128, CH), f32),
            pltpu.VMEM((2, 128, CH), f32),
            dma((8,)), dma((11,)), dma((11,)), dma((2, 8)), dma((2, 8)),
        ],
        compiler_params=pltpu.CompilerParams(
            collective_id=0, has_side_effects=True, vmem_limit_bytes=57 * 1024 * 1024
        ),
        name="scores",
    )(dosage, annotations)


TILES = 64


def stats_kernel(s_ref, t_ref, out_ref, part, got1, sum1, got2, sum2, got3, send, recv):
    w = lax.axis_index("wide")
    g = lax.rem(w, 8)
    h = lax.div(w, 8)

    barrier = pltpu.get_barrier_semaphore()
    for d in range(1, 8):
        pl.semaphore_signal(
            barrier, inc=1, device_id={"wide": w - g + lax.rem(g + d, 8)}, device_id_type=MESH
        )
        pl.semaphore_signal(
            barrier, inc=1, device_id={"wide": lax.rem(h + d, 8) * 8 + g}, device_id_type=MESH
        )

    s = s_ref[...]
    t = t_ref[...]
    ss = split(s)
    ts = split(t)
    part[0:128, :] = dot3(ss, ss, ((1,), (1,)))
    proj = dot3(ss, ts, ((1,), (0,)))
    part[128:256, :] = proj[:, :128]
    part[256:384, :] = proj[:, 128:]
    ones = jnp.ones((8, s.shape[1]), jnp.bfloat16)
    dg = functools.partial(lax.dot_general, preferred_element_type=jnp.float32)
    ssum = dg(ones, ss[0], (((1,), (1,)), ((), ()))) + dg(ones, ss[1], (((1,), (1,)), ((), ())))
    tsum = jnp.sum(t, axis=0, keepdims=True)
    rows = lax.broadcasted_iota(jnp.int32, (8, 128), 0)
    sums = jnp.where(rows == 0, ssum, 0.0)
    sums = jnp.where(rows == 1, tsum[:, :128], sums)
    sums = jnp.where(rows == 2, tsum[:, 128:], sums)
    part[384:392, :] = sums
    part[392:512, :] = jnp.zeros((120, 128), jnp.float32)

    pl.semaphore_wait(barrier, 14)

    def in_block(d):
        return lax.rem(g + d, 8)

    def across(d):
        return lax.rem(h + d, 8)

    def copy1(d):
        p = in_block(d)
        return pltpu.make_async_remote_copy(
            src_ref=part.at[pl.ds(pl.multiple_of(p * 64, 64), 64)],
            dst_ref=got1.at[d - 1],
            send_sem=send.at[0, d],
            recv_sem=recv.at[0, d],
            device_id={"wide": w - g + p},
            device_id_type=MESH,
        )

    def copy2(d):
        p = across(d)
        return pltpu.make_async_remote_copy(
            src_ref=sum1.at[pl.ds(pl.multiple_of(p * 8, 8), 8)],
            dst_ref=got2.at[d - 1],
            send_sem=send.at[1, d],
            recv_sem=recv.at[1, d],
            device_id={"wide": p * 8 + g},
            device_id_type=MESH,
        )

    def copy3(d):
        return pltpu.make_async_remote_copy(
            src_ref=sum2,
            dst_ref=got3.at[pl.ds(pl.multiple_of(h * 8, 8), 8)],
            send_sem=send.at[2, d],
            recv_sem=recv.at[2, d],
            device_id={"wide": across(d) * 8 + g},
            device_id_type=MESH,
        )

    def copy4(d):
        return pltpu.make_async_remote_copy(
            src_ref=got3,
            dst_ref=out_ref.at[pl.ds(pl.multiple_of(g * 64, 64), 64)],
            send_sem=send.at[3, d],
            recv_sem=recv.at[3, d],
            device_id={"wide": w - g + in_block(d)},
            device_id_type=MESH,
        )

    for d in range(1, 8):
        copy1(d).start()
    acc = part[pl.ds(pl.multiple_of(g * 64, 64), 64), :]
    for d in range(1, 8):
        copy1(d).wait_recv()
        acc = acc + got1[d - 1]
    sum1[...] = acc
    for d in range(1, 8):
        copy2(d).start()
    acc = sum1[pl.ds(pl.multiple_of(h * 8, 8), 8), :]
    for d in range(1, 8):
        copy2(d).wait_recv()
        acc = acc + got2[d - 1]
    sum2[...] = acc
    for d in range(1, 8):
        copy3(d).start()
    got3[pl.ds(pl.multiple_of(h * 8, 8), 8), :] = acc
    for d in range(1, 8):
        copy3(d).wait_recv()
    for d in range(1, 8):
        copy4(d).start()
    out_ref[pl.ds(pl.multiple_of(g * 64, 64), 64), :] = got3[...]
    for d in range(1, 8):
        copy4(d).wait_recv()
    for copy in (copy1, copy2, copy3, copy4):
        for d in range(1, 8):
            copy(d).wait_send()


def stats(scores, table):
    f32 = jnp.float32
    return pl.pallas_call(
        stats_kernel,
        out_shape=jax.ShapeDtypeStruct((TILES * 8, 128), f32),
        in_specs=[pl.BlockSpec(memory_space=pltpu.VMEM)] * 2,
        out_specs=pl.BlockSpec(memory_space=pltpu.VMEM),
        scratch_shapes=[
            pltpu.VMEM((TILES * 8, 128), f32),
            pltpu.VMEM((7, 64, 128), f32),
            pltpu.VMEM((64, 128), f32),
            pltpu.VMEM((7, 8, 128), f32),
            pltpu.VMEM((8, 128), f32),
            pltpu.VMEM((64, 128), f32),
            pltpu.SemaphoreType.DMA((4, 8)),
            pltpu.SemaphoreType.DMA((4, 8)),
        ],
        compiler_params=pltpu.CompilerParams(
            collective_id=1, has_side_effects=True, vmem_limit_bytes=32 * 1024 * 1024
        ),
        name="stats",
    )(scores, table)


def finish_kernel(total_variants, p_ref, s_ref, ld_ref, fit_ref):
    n = lax.axis_index("narrow")
    scale = 1.0 / total_variants
    sums = p_ref[384:392, :] * scale
    m_row = sums[0:1, :]
    chi = jnp.concatenate([sums[1:2, :], sums[2:3, :]], axis=1)
    ri = lax.broadcasted_iota(jnp.int32, (128, 128), 0)
    ci = lax.broadcasted_iota(jnp.int32, (128, 128), 1)
    eye = ri == ci
    m_col = jnp.sum(jnp.where(eye, jnp.broadcast_to(m_row, (128, 128)), 0.0), axis=1, keepdims=True)
    cov = p_ref[0:128, :] * scale - m_col * m_row
    proj = jnp.concatenate([p_ref[128:256, :], p_ref[256:384, :]], axis=1) * scale - m_col * chi
    var = jnp.sum(jnp.where(eye, cov, 0.0), axis=1, keepdims=True)
    rstd = 1.0 / jnp.sqrt(var + 1e-05)

    half = ld_ref.shape[1]
    own = s_ref[:, pl.ds(pl.multiple_of(n * half, half), half)]
    ld_ref[...] = (own - m_col) * rstd

    sub = lax.broadcasted_iota(jnp.int32, (8, 1), 0)

    def step(i, carry):
        a, b = carry
        cols = [jnp.broadcast_to(a[:, r : r + 1], (128, 128)) for r in range(8)]
        panel = [c[:8] for c in cols]
        right = [a[:8], b[:8, :128], b[:8, 128:]]
        for r in range(8):
            pivots = [jnp.broadcast_to(c[r : r + 1], (8, 128)) for c in panel]
            inv = 1.0 / pivots[r]
            factor = panel[r]
            here = sub == r
            for c in range(r + 1, 8):
                row = pivots[c] * inv
                panel[c] = jnp.where(here, row, panel[c] - factor * row)
            for k in range(3):
                row = jnp.broadcast_to(right[k][r : r + 1], (8, 128)) * inv
                right[k] = jnp.where(here, row, right[k] - factor * row)
        rest = [a[8:], b[8:, :128], b[8:, 128:]]
        for r in range(8):
            col = cols[r][8:]
            rest = [x - col * y[r : r + 1] for x, y in zip(rest, right)]
        a, b0, b1 = (jnp.concatenate([x, y], axis=0) for x, y in zip(rest, right))
        return pltpu.roll(a, 120, 1), jnp.concatenate([b0, b1], axis=1)

    _, coef = lax.fori_loop(0, 16, step, (cov, proj))
    cs = split(coef)
    rows = 256
    for k in range(fit_ref.shape[0] // rows):
        dev = (s_ref[:, k * rows : (k + 1) * rows] - m_col).T
        fit_ref[k * rows : (k + 1) * rows, :] = chi + dot3(split(dev), cs, ((1,), (0,)))


def finish(totals, scores, traits, total_variants):
    return pl.pallas_call(
        functools.partial(finish_kernel, total_variants),
        out_shape=(
            jax.ShapeDtypeStruct((128, scores.shape[1] // 2), jnp.float32),
            jax.ShapeDtypeStruct((scores.shape[1], traits), jnp.float32),
        ),
        in_specs=[pl.BlockSpec(memory_space=pltpu.VMEM)] * 2,
        out_specs=(pl.BlockSpec(memory_space=pltpu.VMEM),) * 2,
        compiler_params=pltpu.CompilerParams(vmem_limit_bytes=32 * 1024 * 1024),
        name="finish",
    )(totals, scores)


def shards(dosage, annotations, test_statistic_table):
    total_variants = lax.axis_size("wide") * dosage.shape[1]
    scores = strip_scores(dosage, annotations, total_variants)
    totals = stats(scores, test_statistic_table)
    return finish(totals, scores, test_statistic_table.shape[1], total_variants)


def solution(mesh):
    in_specs = (P(None, "wide"), P(None, "wide"), P("wide", "narrow"))
    out_specs = (P(None, ("wide", "narrow")), P("wide", "narrow"))
    return jax.shard_map(shards, mesh=mesh, in_specs=in_specs, out_specs=out_specs, check_vma=False)
```

```python
import functools

import jax
import jax.numpy as jnp
from jax import lax
from jax.experimental import pallas as pl
from jax.experimental.pallas import tpu as pltpu
from jax.sharding import PartitionSpec as P

MESH = pl.DeviceIdType.MESH


def split(x):
    hi = x.astype(jnp.bfloat16)
    return hi, (x - hi.astype(jnp.float32)).astype(jnp.bfloat16)


def dot3(a, b, dims):
    ah, al = a
    bh, bl = b
    dg = functools.partial(
        lax.dot_general, dimension_numbers=(dims, ((), ())), preferred_element_type=jnp.float32
    )
    return dg(ah, bh) + (dg(ah, bl) + dg(al, bh))


CH = 256
ROWS = 144


def scores_kernel(
    total_variants, x_ref, ann_hbm, t_ref, out_hbm, total_ref,
    ann_ref, out_ref, geno, annot, acc, edge_acc, wbuf, edge, cnt, cnt_got, twin_out, twin_got, halo_out, halo_got,
    table, table_hi, table_lo, part, got1, sum1, got2, sum2, got3,
    load_sem, send, recv, csend, crecv, ssend, srecv,
):
    f32 = jnp.float32
    bf16 = jnp.bfloat16
    w = lax.axis_index("wide")
    n = lax.axis_index("narrow")
    wides = lax.axis_size("wide")
    samples = x_ref.shape[0]
    core = lax.rem(w, 2)
    chip = lax.div(w, 2)
    g = lax.rem(w, 8)
    h = lax.div(w, 8)
    groups = wides // 8
    mate = w + 1 - 2 * core
    over = lax.rem(w + 2 * core - 1 + wides, wides)
    left_chip = lax.rem(chip + core - 1 + wides // 2, wides // 2)
    turned = lax.rem(left_chip, 2)
    p = n + turned - 2 * n * turned
    csl = 2 * core + p
    base = 4 * core
    outer = 8 * core
    beside = 8 - 8 * core

    def columns(c, count=1):
        return pl.ds(pl.multiple_of(c * CH, CH), count * CH)

    def inner(i):
        return jnp.where(core == 0, 3 - i, i)

    def device(wide, narrow):
        return {"wide": wide, "narrow": narrow}

    def load(t):
        if t == 0:
            c = outer + csl
        elif t <= 4:
            c = 4 + inner(t - 1)
        else:
            c = outer + lax.rem(csl + t - 4, 4)
        return pltpu.make_async_copy(x_ref.at[:, columns(c - base)], geno.at[:, columns(c)], load_sem.at[t])

    def load_table():
        return pltpu.make_async_copy(t_ref, table, load_sem.at[8])

    def load_annotations():
        return pltpu.make_async_copy(ann_hbm, ann_ref, load_sem.at[9])

    def store_scores():
        return pltpu.make_async_copy(out_ref, out_hbm, load_sem.at[10])

    load(0).start()
    load_annotations().start()
    for t in range(1, 8):
        load(t).start()
    load_table().start()

    barrier = pltpu.get_barrier_semaphore()

    def hello(wide, narrow):
        pl.semaphore_signal(barrier, inc=1, device_id=device(wide, narrow), device_id_type=MESH)

    for d in range(1, 8):
        hello(w - g + lax.rem(g + d, 8), n)
    for d in range(1, groups):
        hello(lax.rem(h + d, groups) * 8 + g, n)
    hello(w, 1 - n)
    hello(over, 0)
    hello(over, 1)

    tail = jnp.where(lax.broadcasted_iota(jnp.int32, (16, CH), 0) == 0, 1.0, 0.0).astype(bf16)
    count = jnp.zeros((8, 128), f32)
    load_annotations().wait()
    for c in range(8):
        a = ann_ref[:, c * CH : (c + 1) * CH].astype(f32).astype(bf16)
        annot[0:128, columns(base + c)] = a
        annot[128:144, columns(base + c)] = tail
        count = count + lax.dot_general(
            jnp.ones((8, CH), bf16), a, (((1,), (1,)), ((), ())), preferred_element_type=f32
        )
    cnt[0] = count
    acc[...] = jnp.zeros_like(acc)
    ri = lax.broadcasted_iota(jnp.int32, (CH, CH), 0)
    ci = lax.broadcasted_iota(jnp.int32, (CH, CH), 1)
    edge[0] = jnp.where(core == 0, 0.5, jnp.where(ci <= ri, 1.0, 0.0))
    edge[1] = jnp.where(core == 1, 0.5, jnp.where(ri <= ci, 1.0, 0.0))

    def remote(src, dst, s, r, wide, narrow):
        return pltpu.make_async_remote_copy(
            src_ref=src, dst_ref=dst, send_sem=s, recv_sem=r,
            device_id=device(wide, narrow), device_id_type=MESH,
        )

    def count1(d):
        return remote(
            cnt.at[0], cnt_got.at[0, d], csend.at[0, d], crecv.at[0, d],
            w - g + lax.rem(g + d, 8), n,
        )

    def count2(d):
        return remote(
            cnt.at[1], cnt_got.at[1, d], csend.at[1, d], crecv.at[1, d],
            lax.rem(h + d, groups) * 8 + g, n,
        )

    eps = 1e-05

    def standardize(c):
        at = columns(c)
        block = 256

        def rows(i):
            return pl.ds(pl.multiple_of(i * block, block), block)

        pivot = geno[0:16, at].astype(f32)[0:1]

        def sums(i, s):
            x = (geno[rows(i), at].astype(f32) - pivot).reshape(block // 8, 8, CH)
            return s[0] + jnp.sum(x, axis=0), s[1] + jnp.sum(x * x, axis=0)

        zero = jnp.zeros((8, CH), f32)
        first, second = lax.fori_loop(0, samples // block, sums, (zero, zero))
        shift = jnp.sum(first, axis=0, keepdims=True) / samples
        var = jnp.sum(second, axis=0, keepdims=True) / samples - shift * shift
        mean = pivot + shift
        inv = 1.0 / jnp.sqrt(jnp.maximum(var, 0.0) + eps)

        def put(i, _):
            geno[rows(i), at] = ((geno[rows(i), at].astype(f32) - mean) * inv).astype(bf16)
            return 0

        lax.fori_loop(0, samples // block, put, 0)

    def halo_geno():
        return remote(
            geno.at[:, columns(outer + csl)], geno.at[:, columns(12)], send.at[0], recv.at[0], over, p
        )

    def halo_annot():
        return remote(
            annot.at[:, columns(outer + csl)], annot.at[:, columns(12)], send.at[1], recv.at[1], over, p
        )

    def mate_geno(q):
        return remote(
            geno.at[:, columns(4 + q)], geno.at[:, columns(outer + q)],
            send.at[2 + q], recv.at[2 + q], mate, n,
        )

    def mate_geno_from(q):
        return remote(
            geno.at[:, columns(4 + q)], geno.at[:, columns(beside + q)],
            send.at[2 + q], recv.at[2 + q], mate, n,
        )

    def mate_annot():
        return remote(
            annot.at[:, columns(4, 4)], annot.at[:, columns(outer, 4)], send.at[6], recv.at[6], mate, n
        )

    def mate_annot_from():
        return remote(
            annot.at[:, columns(4, 4)], annot.at[:, columns(beside, 4)], send.at[6], recv.at[6], mate, n
        )

    load(0).wait()
    standardize(outer + csl)
    pl.semaphore_wait(barrier, 7 + groups - 1 + 3)
    halo_geno().start()
    halo_annot().start()
    mate_annot().start()
    for d in range(1, 8):
        count1(d).start()
    for q in range(4):
        load(1 + q).wait()

    def mate_step(i, _):
        standardize(4 + inner(i))
        mate_geno(inner(i)).start()
        return 0

    lax.fori_loop(0, 4, mate_step, 0)
    for t in range(5, 8):
        load(t).wait()

    def rest_step(t, _):
        standardize(outer + lax.rem(csl + t, 4))
        return 0

    lax.fori_loop(1, 4, rest_step, 0)
    load_table().wait()
    table_hi[...], table_lo[...] = split(table[...])
    table_sum = jnp.sum(table[...], axis=0, keepdims=True)

    total_count = cnt[0]
    for d in range(1, 8):
        count1(d).wait_recv()
        total_count = total_count + cnt_got[0, d]
    cnt[1] = total_count
    for d in range(1, groups):
        count2(d).start()

    k1 = (1.0 + 1.0 / (samples - 2)) / (float(samples) * samples)
    k2 = 1.0 / (samples - 2)
    diff = (
        lax.broadcasted_iota(jnp.int32, (CH, CH), 0) - lax.broadcasted_iota(jnp.int32, (CH, CH), 1)
    ).astype(f32)

    def correlate(own, other):
        products = lax.dot_general(
            geno[:, columns(own)], geno[:, columns(other)], (((0,), (0,)), ((), ())),
            preferred_element_type=f32,
        )
        return (products * products) * k1 - k2

    def place(t):
        return jnp.where(core == 0, t, 7 - t), jnp.where(core == 0, t, 11 - t)

    def weigh(t):
        own, other = place(t)
        for b in range(5):
            value = correlate(own + b, other)
            if b in (0, 4):
                value = value * edge[b // 4]
            wbuf[lax.rem(t, 2), b * CH : (b + 1) * CH, :] = value.astype(bf16)

    def apply(t):
        own, other = place(t)
        weights = wbuf[lax.rem(t, 2)]
        acc[:, columns(other)] += jnp.dot(
            annot[:, columns(own, 5)], weights, preferred_element_type=f32
        )
        acc[:, columns(own, 5)] += lax.dot_general(
            annot[:, columns(other)], weights, (((1,), (1,)), ((), ())), preferred_element_type=f32
        )

    def step(t, _):
        apply(t - 1)
        weigh(t)
        return 0

    def inner_late(t):
        return jnp.where(core == 0, t - 4, 7 - t)

    def late_step(t, _):
        mate_geno_from(inner_late(t)).wait_recv()
        return step(t, 0)

    weigh(jnp.int32(0))
    lax.fori_loop(1, 4, step, 0)
    total_count = cnt[1]
    for d in range(1, groups):
        count2(d).wait_recv()
        total_count = total_count + cnt_got[1, d]
    halo_annot().wait_recv()
    halo_geno().wait_recv()
    apply(jnp.int32(3))
    open_end = jnp.where(core == 0, w == 0, w == wides - 1)
    near = jnp.where(open_end, 8192, jnp.where(core == 0, -8192, CH * n))
    far = jnp.where(core == 0, 512 + CH * n, 8192)
    first_row = jnp.where(core == 0, 512, 0)
    for b in range(4):
        row = ri + b * CH
        diff = row - ci
        inside = (diff >= near) & (diff <= far) & (row >= first_row)
        value = jnp.where(inside, correlate(outer + b, 12), 0.0)
        wbuf[0, b * CH : (b + 1) * CH, :] = value.astype(bf16)
    weights = wbuf[0, 0 : 4 * CH, :]
    acc[:, columns(12)] = jnp.dot(
        annot[:, columns(outer, 4)], weights, preferred_element_type=f32
    )
    edge_acc[...] = lax.dot_general(
        annot[:, columns(12)], weights, (((1,), (1,)), ((), ())), preferred_element_type=f32
    )

    eye = ri[:128, :128] == ci[:128, :128]
    counts = jnp.sum(
        jnp.where(eye, jnp.broadcast_to(total_count[0:1, :], (128, 128)), 0.0),
        axis=1, keepdims=True,
    )
    shares = counts / total_variants
    zero_value = (0.0 - shares).astype(bf16).astype(f32)
    step_value = (1.0 - shares).astype(bf16).astype(f32) - zero_value

    def centred(sums):
        return zero_value * sums[128:129, :] + step_value * sums[0:128, :]

    def halo_back(m):
        return remote(
            halo_out, halo_got.at[n], send.at[7 + m], recv.at[7 + n], over, m
        )

    def halo_back_from(m):
        return remote(
            halo_out, halo_got.at[m], send.at[7 + m], recv.at[7 + m], over, m
        )

    def twin(part):
        return remote(
            twin_out.at[pl.ds(2 * part, 2)], twin_got.at[pl.ds(2 * part, 2)],
            send.at[9 + part], recv.at[9 + part], w, 1 - n,
        )

    halo_out[...] = centred(acc[:, columns(12)]).astype(bf16)
    for m in range(2):
        halo_back(m).start()
    for q in range(4):
        twin_out[q] = centred(edge_acc[:, q * CH : (q + 1) * CH]).astype(bf16)
    twin(1).start()

    @pl.when(core == 1)
    def _():
        twin(0).start()

    @pl.when(core == 0)
    def _():
        twin_got[0:2] = jnp.zeros((2, 128, CH), bf16)

    mate_annot_from().wait_recv()
    mate_geno_from(inner_late(4)).wait_recv()
    weigh(jnp.int32(4))
    lax.fori_loop(5, 8, late_step, 0)
    apply(jnp.int32(7))

    def out(c):
        return columns(c - base)

    for q in range(4):
        out_ref[:, out(4 + q)] = centred(acc[:, columns(4 + q)])
        out_ref[:, out(outer + q)] = centred(
            acc[:, columns(outer + q)] + edge_acc[:, q * CH : (q + 1) * CH]
        )
    for m in range(2):
        halo_back_from(m).wait_recv()
        out_ref[:, out(outer + 2 * core + m)] += halo_got[m].astype(f32)
    twin(1).wait_recv()

    @pl.when(core == 1)
    def _():
        twin(0).wait_recv()

    for q in range(4):
        out_ref[:, out(outer + q)] += twin_got[q].astype(f32)

    store_scores().start()
    dg = functools.partial(lax.dot_general, preferred_element_type=f32)
    scores = split(out_ref[...])
    proj = dot3(scores, (table_hi[...], table_lo[...]), ((1,), (0,)))
    part[96:224, :] = proj[:, :128]
    part[224:352, :] = proj[:, 128:]
    cross = dot3(scores, scores, ((1,), (1,)))
    low = lax.broadcasted_iota(jnp.int32, (64, 128), 1) < 64
    part[0:64, :] = jnp.where(low, cross[:64], cross[64:])
    part[64:96, :] = jnp.where(low[:32], pltpu.roll(cross[0:32], 64, 1), cross[32:64])
    ones = jnp.ones((8, 8 * CH), bf16)
    by_lane = (((1,), (1,)), ((), ()))
    score_sum = dg(ones, scores[0], by_lane) + dg(ones, scores[1], by_lane)
    line = lax.broadcasted_iota(jnp.int32, (8, 128), 0)
    sums = jnp.where(line == 0, score_sum, 0.0)
    sums = jnp.where(line == 1, table_sum[:, :128], sums)
    sums = jnp.where(line == 2, table_sum[:, 128:], sums)
    part[352:360, :] = sums
    part[360:384, :] = jnp.zeros((24, 128), f32)

    def in_block(d):
        return lax.rem(g + d, 8)

    def across(d):
        return lax.rem(h + d, groups)

    def piece(i, size):
        return pl.ds(pl.multiple_of(i * size, size), size)

    def copy1(d):
        return remote(
            part.at[piece(in_block(d), 48)], got1.at[d - 1], ssend.at[0, d], srecv.at[0, d],
            w - g + in_block(d), n,
        )

    def copy2(d):
        return remote(
            sum1.at[piece(across(d), 8)], got2.at[d - 1], ssend.at[1, d], srecv.at[1, d],
            across(d) * 8 + g, n,
        )

    def copy3(d):
        return remote(
            sum2, got3.at[piece(h, 8)], ssend.at[2, d], srecv.at[2, d], across(d) * 8 + g, n
        )

    def copy3_from(d):
        return remote(
            sum2, got3.at[piece(lax.rem(h - d + groups, groups), 8)],
            ssend.at[2, d], srecv.at[2, d], across(d) * 8 + g, n,
        )

    def copy4(d):
        return remote(
            got3.at[pl.ds(0, 48)], total_ref.at[piece(g, 48)], ssend.at[3, d], srecv.at[3, d],
            w - g + in_block(d), n,
        )

    def copy4_from(d):
        return remote(
            got3.at[pl.ds(0, 48)], total_ref.at[piece(lax.rem(g - d + 8, 8), 48)],
            ssend.at[3, d], srecv.at[3, d], w - g + in_block(d), n,
        )

    for d in range(1, 8):
        copy1(d).start()
    total = part[piece(g, 48), :]
    for d in range(1, 8):
        copy1(d).wait_recv()
        total = total + got1[d - 1]
    sum1[0:48, :] = total
    sum1[48:64, :] = jnp.zeros((16, 128), f32)
    for d in range(1, groups):
        copy2(d).start()
    total = sum1[piece(h, 8), :]
    for d in range(1, groups):
        copy2(d).wait_recv()
        total = total + got2[d - 1]
    sum2[...] = total
    for d in range(1, groups):
        copy3(d).start()
    got3[piece(h, 8), :] = total
    for d in range(1, groups):
        copy3_from(d).wait_recv()
    for d in range(1, 8):
        copy4(d).start()
    total_ref[piece(g, 48), :] = got3[0:48, :]
    for d in range(1, 8):
        copy4_from(d).wait_recv()
    for d in range(1, 8):
        copy1(d).wait_send()
        copy4(d).wait_send()
    for d in range(1, groups):
        copy2(d).wait_send()
        copy3(d).wait_send()

    store_scores().wait()
    for d in range(1, 8):
        count1(d).wait_send()
    for d in range(1, groups):
        count2(d).wait_send()
    halo_geno().wait_send()
    halo_annot().wait_send()
    mate_annot().wait_send()
    for q in range(4):
        mate_geno(q).wait_send()
    for m in range(2):
        halo_back(m).wait_send()
    twin(1).wait_send()

    @pl.when(core == 1)
    def _():
        twin(0).wait_send()


def strip_scores(dosage, annotations, table, total_variants):
    f32 = jnp.float32
    bf16 = jnp.bfloat16
    samples = dosage.shape[0]
    dma = pltpu.SemaphoreType.DMA
    hbm = pl.BlockSpec(memory_space=pltpu.HBM)
    vmem = pl.BlockSpec(memory_space=pltpu.VMEM)
    return pl.pallas_call(
        functools.partial(scores_kernel, total_variants),
        out_shape=(
            jax.ShapeDtypeStruct((128, 8 * CH), f32),
            jax.ShapeDtypeStruct((384, 128), f32),
        ),
        in_specs=[hbm, hbm, hbm],
        out_specs=(hbm, vmem),
        scratch_shapes=[
            pltpu.VMEM(annotations.shape, jnp.int32),
            pltpu.VMEM((128, 8 * CH), f32),
            pltpu.VMEM((samples, 13 * CH), bf16),
            pltpu.VMEM((ROWS, 13 * CH), bf16),
            pltpu.VMEM((ROWS, 13 * CH), f32),
            pltpu.VMEM((ROWS, 4 * CH), f32),
            pltpu.VMEM((2, 5 * CH, CH), bf16),
            pltpu.VMEM((2, CH, CH), f32),
            pltpu.VMEM((2, 8, 128), f32),
            pltpu.VMEM((2, 8, 8, 128), f32),
            pltpu.VMEM((4, 128, CH), bf16),
            pltpu.VMEM((4, 128, CH), bf16),
            pltpu.VMEM((128, CH), bf16),
            pltpu.VMEM((2, 128, CH), bf16),
            pltpu.VMEM(table.shape, f32),
            pltpu.VMEM(table.shape, bf16),
            pltpu.VMEM(table.shape, bf16),
            pltpu.VMEM((384, 128), f32),
            pltpu.VMEM((7, 48, 128), f32),
            pltpu.VMEM((64, 128), f32),
            pltpu.VMEM((7, 8, 128), f32),
            pltpu.VMEM((8, 128), f32),
            pltpu.VMEM((64, 128), f32),
            dma((11,)), dma((11,)), dma((11,)), dma((2, 8)), dma((2, 8)), dma((4, 8)), dma((4, 8)),
        ],
        compiler_params=pltpu.CompilerParams(
            collective_id=0, has_side_effects=True, vmem_limit_bytes=60 * 1024 * 1024
        ),
        name="scores",
    )(dosage, annotations, table)


def finish_kernel(total_variants, p_ref, s_hbm, ld_ref, fit_ref, s_ref, sem):
    n = lax.axis_index("narrow")
    fetch = pltpu.make_async_copy(s_hbm, s_ref, sem)
    fetch.start()
    scale = 1.0 / total_variants
    sums = p_ref[352:360, :] * scale
    m_row = sums[0:1, :]
    chi = jnp.concatenate([sums[1:2, :], sums[2:3, :]], axis=1)
    ri = lax.broadcasted_iota(jnp.int32, (128, 128), 0)
    ci = lax.broadcasted_iota(jnp.int32, (128, 128), 1)
    eye = ri == ci
    m_col = jnp.sum(jnp.where(eye, jnp.broadcast_to(m_row, (128, 128)), 0.0), axis=1, keepdims=True)
    low = ci[:64] < 64
    pair = p_ref[0:64, :]
    above = p_ref[64:96, :]
    above = jnp.concatenate([pltpu.roll(above, 64, 1), above], axis=0)
    zeros = jnp.zeros((64, 128), jnp.float32)
    above_only = jnp.concatenate([jnp.where(low, zeros, above), zeros], axis=0)
    cross = jnp.concatenate([jnp.where(low, pair, above), jnp.where(low, zeros, pair)], axis=0)
    cov = (cross + above_only.T) * scale - m_col * m_row
    proj = jnp.concatenate([p_ref[96:224, :], p_ref[224:352, :]], axis=1) * scale - m_col * chi
    var = jnp.sum(jnp.where(eye, cov, 0.0), axis=1, keepdims=True)
    rstd = 1.0 / jnp.sqrt(var + 1e-05)

    sub = lax.broadcasted_iota(jnp.int32, (8, 1), 0)

    def step(i, carry):
        a, b = carry
        cols = [jnp.broadcast_to(a[:, r : r + 1], (128, 128)) for r in range(8)]
        panel = [c[:8] for c in cols]
        right = [a[:8], b[:8, :128], b[:8, 128:]]
        for r in range(8):
            pivots = [jnp.broadcast_to(c[r : r + 1], (8, 128)) for c in panel]
            inv = 1.0 / pivots[r]
            factor = panel[r]
            here = sub == r
            for c in range(r + 1, 8):
                row = pivots[c] * inv
                panel[c] = jnp.where(here, row, panel[c] - factor * row)
            for k in range(3):
                row = jnp.broadcast_to(right[k][r : r + 1], (8, 128)) * inv
                right[k] = jnp.where(here, row, right[k] - factor * row)
        rest = [a[8:], b[8:, :128], b[8:, 128:]]
        for r in range(8):
            col = cols[r][8:]
            rest = [x - col * y[r : r + 1] for x, y in zip(rest, right)]
        a, b0, b1 = (jnp.concatenate([x, y], axis=0) for x, y in zip(rest, right))
        return pltpu.roll(a, 120, 1), jnp.concatenate([b0, b1], axis=1)

    _, coef = lax.fori_loop(0, 16, step, (cov, proj))
    fetch.wait()
    half = ld_ref.shape[1]
    own = s_ref[:, pl.ds(pl.multiple_of(n * half, half), half)]
    ld_ref[...] = (own - m_col) * rstd
    cs = split(coef)
    rows = 256
    for k in range(fit_ref.shape[0] // rows):
        dev = (s_ref[:, k * rows : (k + 1) * rows] - m_col).T
        fit_ref[k * rows : (k + 1) * rows, :] = chi + dot3(split(dev), cs, ((1,), (0,)))


def finish(totals, scores, traits, total_variants):
    return pl.pallas_call(
        functools.partial(finish_kernel, total_variants),
        out_shape=(
            jax.ShapeDtypeStruct((128, scores.shape[1] // 2), jnp.float32),
            jax.ShapeDtypeStruct((scores.shape[1], traits), jnp.float32),
        ),
        in_specs=[
            pl.BlockSpec(memory_space=pltpu.VMEM), pl.BlockSpec(memory_space=pltpu.HBM)
        ],
        out_specs=(pl.BlockSpec(memory_space=pltpu.VMEM),) * 2,
        scratch_shapes=[pltpu.VMEM(scores.shape, jnp.float32), pltpu.SemaphoreType.DMA],
        compiler_params=pltpu.CompilerParams(vmem_limit_bytes=60 * 1024 * 1024),
        name="finish",
    )(totals, scores)


def shards(dosage, annotations, test_statistic_table):
    total_variants = lax.axis_size("wide") * dosage.shape[1]
    scores, totals = strip_scores(dosage, annotations, test_statistic_table, total_variants)
    return finish(totals, scores, test_statistic_table.shape[1], total_variants)


def solution(mesh):
    in_specs = (P(None, "wide"), P(None, "wide"), P("wide", "narrow"))
    out_specs = (P(None, ("wide", "narrow")), P("wide", "narrow"))
    return jax.shard_map(shards, mesh=mesh, in_specs=in_specs, out_specs=out_specs, check_vma=False)
```

```python
import functools

import jax
import jax.numpy as jnp
from jax import lax
from jax.experimental import pallas as pl
from jax.experimental.pallas import tpu as pltpu
from jax.sharding import PartitionSpec as P

MESH = pl.DeviceIdType.MESH


def split(x):
    hi = x.astype(jnp.bfloat16)
    return hi, (x - hi.astype(jnp.float32)).astype(jnp.bfloat16)


def dot3(a, b, dims):
    ah, al = a
    bh, bl = b
    dg = functools.partial(
        lax.dot_general, dimension_numbers=(dims, ((), ())), preferred_element_type=jnp.float32
    )
    return dg(ah, bh) + (dg(ah, bl) + dg(al, bh))


CH = 256
ROWS = 144
PER_CORE = 23


def scores_kernel(
    total_variants, x_ref, ann_hbm, t_ref, out_hbm, total_ref,
    ann_ref, out_ref, geno, annot, acc, edge_acc, wbuf, edge, cnt, cnt_got, twin_out, twin_got, halo_out, halo_got,
    table, table_hi, table_lo, part, got_half, half_sum, got_tiles, tile_sum,
    load_sem, send, recv, csend, crecv, ssend, srecv,
):
    f32 = jnp.float32
    bf16 = jnp.bfloat16
    w = lax.axis_index("wide")
    n = lax.axis_index("narrow")
    wides = lax.axis_size("wide")
    samples = x_ref.shape[0]
    core = lax.rem(w, 2)
    chip = lax.div(w, 2)
    g = lax.rem(w, 8)
    h = lax.div(w, 8)
    groups = wides // 8
    chips = wides // 2
    mate = w + 1 - 2 * core
    over = lax.rem(w + 2 * core - 1 + wides, wides)
    left_chip = lax.rem(chip + core - 1 + wides // 2, wides // 2)
    turned = lax.rem(left_chip, 2)
    p = n + turned - 2 * n * turned
    csl = 2 * core + p
    base = 4 * core
    outer = 8 * core
    beside = 8 - 8 * core

    def columns(c, count=1):
        return pl.ds(pl.multiple_of(c * CH, CH), count * CH)

    def inner(i):
        return jnp.where(core == 0, 3 - i, i)

    def device(wide, narrow):
        return {"wide": wide, "narrow": narrow}

    def load(t):
        if t == 0:
            c = outer + csl
        elif t <= 4:
            c = 4 + inner(t - 1)
        else:
            c = outer + lax.rem(csl + t - 4, 4)
        return pltpu.make_async_copy(x_ref.at[:, columns(c - base)], geno.at[:, columns(c)], load_sem.at[t])

    def load_table():
        return pltpu.make_async_copy(t_ref, table, load_sem.at[8])

    def load_annotations():
        return pltpu.make_async_copy(ann_hbm, ann_ref, load_sem.at[9])

    def store_scores():
        return pltpu.make_async_copy(out_ref, out_hbm, load_sem.at[10])

    load(0).start()
    load_annotations().start()
    for t in range(1, 8):
        load(t).start()
    load_table().start()

    twin_got[...] = jnp.zeros(twin_got.shape, bf16)
    barrier = pltpu.get_barrier_semaphore()

    def hello(wide, narrow):
        pl.semaphore_signal(barrier, inc=1, device_id=device(wide, narrow), device_id_type=MESH)

    for d in range(1, 8):
        hello(w - g + lax.rem(g + d, 8), n)

    def hello_chip(d, _):
        hello(lax.rem(w + 2 * d, wides), n)
        return 0

    lax.fori_loop(1, chips, hello_chip, 0)
    hello(w, 1 - n)
    hello(over, 0)
    hello(over, 1)

    tail = jnp.where(lax.broadcasted_iota(jnp.int32, (16, CH), 0) == 0, 1.0, 0.0).astype(bf16)
    count = jnp.zeros((8, 128), f32)
    load_annotations().wait()
    for c in range(8):
        a = ann_ref[:, c * CH : (c + 1) * CH].astype(f32).astype(bf16)
        annot[0:128, columns(base + c)] = a
        annot[128:144, columns(base + c)] = tail
        count = count + lax.dot_general(
            jnp.ones((8, CH), bf16), a, (((1,), (1,)), ((), ())), preferred_element_type=f32
        )
    cnt[0] = count
    acc[...] = jnp.zeros_like(acc)
    ri = lax.broadcasted_iota(jnp.int32, (CH, CH), 0)
    ci = lax.broadcasted_iota(jnp.int32, (CH, CH), 1)
    edge[0] = jnp.where(core == 0, 0.5, jnp.where(ci <= ri, 1.0, 0.0))
    edge[1] = jnp.where(core == 1, 0.5, jnp.where(ri <= ci, 1.0, 0.0))

    def remote(src, dst, s, r, wide, narrow):
        return pltpu.make_async_remote_copy(
            src_ref=src, dst_ref=dst, send_sem=s, recv_sem=r,
            device_id=device(wide, narrow), device_id_type=MESH,
        )

    def count1(d):
        return remote(
            cnt.at[0], cnt_got.at[0, d], csend.at[0, d], crecv.at[0, d],
            w - g + lax.rem(g + d, 8), n,
        )

    def count2(d):
        return remote(
            cnt.at[1], cnt_got.at[1, d], csend.at[1, d], crecv.at[1, d],
            lax.rem(h + d, groups) * 8 + g, n,
        )

    eps = 1e-05

    def standardize(c):
        at = columns(c)
        block = 256

        def rows(i):
            return pl.ds(pl.multiple_of(i * block, block), block)

        pivot = geno[0:16, at].astype(f32)[0:1]

        def sums(i, s):
            x = (geno[rows(i), at].astype(f32) - pivot).reshape(block // 8, 8, CH)
            return s[0] + jnp.sum(x, axis=0), s[1] + jnp.sum(x * x, axis=0)

        zero = jnp.zeros((8, CH), f32)
        first, second = lax.fori_loop(0, samples // block, sums, (zero, zero))
        shift = jnp.sum(first, axis=0, keepdims=True) / samples
        var = jnp.sum(second, axis=0, keepdims=True) / samples - shift * shift
        mean = pivot + shift
        inv = 1.0 / jnp.sqrt(jnp.maximum(var, 0.0) + eps)

        def put(i, _):
            geno[rows(i), at] = ((geno[rows(i), at].astype(f32) - mean) * inv).astype(bf16)
            return 0

        lax.fori_loop(0, samples // block, put, 0)

    def halo_geno():
        return remote(
            geno.at[:, columns(outer + csl)], geno.at[:, columns(12)], send.at[0], recv.at[0], over, p
        )

    def halo_annot():
        return remote(
            annot.at[:, columns(outer + csl)], annot.at[:, columns(12)], send.at[1], recv.at[1], over, p
        )

    def mate_geno(q):
        return remote(
            geno.at[:, columns(4 + q)], geno.at[:, columns(outer + q)],
            send.at[2 + q], recv.at[2 + q], mate, n,
        )

    def mate_geno_from(q):
        return remote(
            geno.at[:, columns(4 + q)], geno.at[:, columns(beside + q)],
            send.at[2 + q], recv.at[2 + q], mate, n,
        )

    def mate_annot():
        return remote(
            annot.at[:, columns(4, 4)], annot.at[:, columns(outer, 4)], send.at[6], recv.at[6], mate, n
        )

    def mate_annot_from():
        return remote(
            annot.at[:, columns(4, 4)], annot.at[:, columns(beside, 4)], send.at[6], recv.at[6], mate, n
        )

    load(0).wait()
    standardize(outer + csl)
    pl.semaphore_wait(barrier, 7 + chips - 1 + 3)
    halo_geno().start()
    halo_annot().start()
    mate_annot().start()
    for d in range(1, 8):
        count1(d).start()
    for q in range(4):
        load(1 + q).wait()

    def mate_step(i, _):
        standardize(4 + inner(i))
        mate_geno(inner(i)).start()
        return 0

    lax.fori_loop(0, 4, mate_step, 0)
    for t in range(5, 8):
        load(t).wait()

    def rest_step(t, _):
        standardize(outer + lax.rem(csl + t, 4))
        return 0

    lax.fori_loop(1, 4, rest_step, 0)
    load_table().wait()
    table_hi[...], table_lo[...] = split(table[...])
    table_sum = jnp.sum(table[...], axis=0, keepdims=True)

    total_count = cnt[0]
    for d in range(1, 8):
        count1(d).wait_recv()
        total_count = total_count + cnt_got[0, d]
    cnt[1] = total_count
    for d in range(1, groups):
        count2(d).start()

    k1 = (1.0 + 1.0 / (samples - 2)) / (float(samples) * samples)
    k2 = 1.0 / (samples - 2)
    diff = (
        lax.broadcasted_iota(jnp.int32, (CH, CH), 0) - lax.broadcasted_iota(jnp.int32, (CH, CH), 1)
    ).astype(f32)

    def correlate(own, other):
        products = lax.dot_general(
            geno[:, columns(own)], geno[:, columns(other)], (((0,), (0,)), ((), ())),
            preferred_element_type=f32,
        )
        return (products * products) * k1 - k2

    def place(t):
        return jnp.where(core == 0, t, 7 - t), jnp.where(core == 0, t, 11 - t)

    def weigh(t):
        own, other = place(t)
        for b in range(5):
            value = correlate(own + b, other)
            if b in (0, 4):
                value = value * edge[b // 4]
            wbuf[lax.rem(t, 2), b * CH : (b + 1) * CH, :] = value.astype(bf16)

    def apply(t):
        own, other = place(t)
        weights = wbuf[lax.rem(t, 2)]
        acc[:, columns(other)] += jnp.dot(
            annot[:, columns(own, 5)], weights, preferred_element_type=f32
        )
        acc[:, columns(own, 5)] += lax.dot_general(
            annot[:, columns(other)], weights, (((1,), (1,)), ((), ())), preferred_element_type=f32
        )

    def step(t, _):
        apply(t - 1)
        weigh(t)
        return 0

    def inner_late(t):
        return jnp.where(core == 0, t - 4, 7 - t)

    def late_step(t, _):
        mate_geno_from(inner_late(t)).wait_recv()
        return step(t, 0)

    weigh(jnp.int32(0))
    lax.fori_loop(1, 4, step, 0)
    mate_annot_from().wait_recv()
    total_count = cnt[1]
    for d in range(1, groups):
        count2(d).wait_recv()
        total_count = total_count + cnt_got[1, d]
    halo_annot().wait_recv()
    halo_geno().wait_recv()
    apply(jnp.int32(3))
    open_end = jnp.where(core == 0, w == 0, w == wides - 1)
    near = jnp.where(open_end, 8192, jnp.where(core == 0, -8192, CH * n))
    far = jnp.where(core == 0, 512 + CH * n, 8192)
    first_row = jnp.where(core == 0, 512, 0)
    for b in range(4):
        row = ri + b * CH
        diff = row - ci
        inside = (diff >= near) & (diff <= far) & (row >= first_row)
        value = jnp.where(inside, correlate(outer + b, 12), 0.0)
        wbuf[0, b * CH : (b + 1) * CH, :] = value.astype(bf16)
    weights = wbuf[0, 0 : 4 * CH, :]
    acc[:, columns(12)] = jnp.dot(
        annot[:, columns(outer, 4)], weights, preferred_element_type=f32
    )
    edge_acc[...] = lax.dot_general(
        annot[:, columns(12)], weights, (((1,), (1,)), ((), ())), preferred_element_type=f32
    )

    eye = ri[:128, :128] == ci[:128, :128]
    counts = jnp.sum(
        jnp.where(eye, jnp.broadcast_to(total_count[0:1, :], (128, 128)), 0.0),
        axis=1, keepdims=True,
    )
    shares = counts / total_variants
    zero_value = (0.0 - shares).astype(bf16).astype(f32)
    step_value = (1.0 - shares).astype(bf16).astype(f32) - zero_value

    def centred(sums):
        return zero_value * sums[128:129, :] + step_value * sums[0:128, :]

    def halo_back(m):
        return remote(
            halo_out, halo_got.at[n], send.at[7 + m], recv.at[7 + n], over, m
        )

    def halo_back_from(m):
        return remote(
            halo_out, halo_got.at[m], send.at[7 + m], recv.at[7 + m], over, m
        )

    def twin(q):
        return remote(
            twin_out.at[q], twin_got.at[q], send.at[9 + q], recv.at[9 + q], w, 1 - n
        )

    twin_sends = ((core == 1) & (n == 0), core == 1, None, (core == 1) | (n == 1))
    twin_gets = ((core == 1) & (n == 1), core == 1, None, (core == 1) | (n == 0))

    def where(conditions, q, act):
        if conditions[q] is None:
            act()
        else:
            pl.when(conditions[q])(act)

    halo_out[...] = centred(acc[:, columns(12)]).astype(bf16)
    for m in range(2):
        halo_back(m).start()
    for q in range(4):
        twin_out[q] = centred(edge_acc[:, q * CH : (q + 1) * CH]).astype(bf16)
    for q in range(4):
        where(twin_sends, q, twin(q).start)

    mate_geno_from(inner_late(4)).wait_recv()
    weigh(jnp.int32(4))
    lax.fori_loop(5, 8, late_step, 0)
    apply(jnp.int32(7))

    def out(c):
        return columns(c - base)

    for q in range(4):
        out_ref[:, out(4 + q)] = centred(acc[:, columns(4 + q)])
        out_ref[:, out(outer + q)] = centred(
            acc[:, columns(outer + q)] + edge_acc[:, q * CH : (q + 1) * CH]
        )
    for m in range(2):
        halo_back_from(m).wait_recv()
        out_ref[:, out(outer + 2 * core + m)] += halo_got[m].astype(f32)
    for q in range(4):
        where(twin_gets, q, twin(q).wait_recv)
    for q in range(4):
        out_ref[:, out(outer + q)] += twin_got[q].astype(f32)

    store_scores().start()
    dg = functools.partial(lax.dot_general, preferred_element_type=f32)
    scores = split(out_ref[...])
    proj = dot3(scores, (table_hi[...], table_lo[...]), ((1,), (0,)))
    part[96:224, :] = proj[:, :128]
    part[224:352, :] = proj[:, 128:]
    cross = dot3(scores, scores, ((1,), (1,)))
    low = lax.broadcasted_iota(jnp.int32, (64, 128), 1) < 64
    part[0:64, :] = jnp.where(low, cross[:64], cross[64:])
    part[64:96, :] = jnp.where(low[:32], pltpu.roll(cross[0:32], 64, 1), cross[32:64])
    ones = jnp.ones((8, 8 * CH), bf16)
    by_lane = (((1,), (1,)), ((), ()))
    score_sum = dg(ones, scores[0], by_lane) + dg(ones, scores[1], by_lane)
    line = lax.broadcasted_iota(jnp.int32, (8, 128), 0)
    sums = jnp.where(line == 0, score_sum, 0.0)
    sums = jnp.where(line == 1, table_sum[:, :128], sums)
    sums = jnp.where(line == 2, table_sum[:, 128:], sums)
    part[352:360, :] = sums
    part[360:368, :] = jnp.zeros((8, 128), f32)

    half_rows = PER_CORE * 8

    def tile(i):
        return pl.ds(pl.multiple_of(i * 8, 8), 8)

    def half_of(c):
        return pl.ds(pl.multiple_of(c * half_rows, 8), half_rows)

    swap = remote(part.at[half_of(1 - core)], got_half, ssend.at[0], srecv.at[0], mate, n)
    swap.start()
    swap.wait_recv()
    half_sum[...] = part[half_of(core), :] + got_half[...]

    def scatter(d, _):
        q = lax.rem(chip + d, chips)

        @pl.when(q < PER_CORE)
        def _():
            remote(
                half_sum.at[tile(q)], got_tiles.at[d - 1], ssend.at[1], srecv.at[1], 2 * q + core, n
            ).start()

        return 0

    lax.fori_loop(1, chips, scatter, 0)
    mine = core * PER_CORE + chip
    all_tiles = remote(got_tiles, got_tiles, ssend.at[1], srecv.at[1], mate, n)

    def tiles(count, i):
        ref = total_ref.at[pl.ds(0, count * 8)]
        return remote(ref, ref, ssend.at[i], srecv.at[i], mate, n)

    def for_others(act):
        pl.when(chip < PER_CORE)(lambda: act(PER_CORE - 1))
        pl.when(chip >= PER_CORE)(lambda: act(PER_CORE))

    def hand_out(d, _):
        q = lax.rem(chip + d, chips)
        remote(
            tile_sum, total_ref.at[tile(mine)], ssend.at[2], srecv.at[2], 2 * q + core, n
        ).start()
        return 0

    @pl.when(chip < PER_CORE)
    def _():
        all_tiles.wait_recv()
        total = half_sum[tile(chip), :] + jnp.sum(got_tiles[...], axis=0)
        tile_sum[...] = total
        lax.fori_loop(1, chips, hand_out, 0)
        total_ref[tile(mine), :] = total

    for_others(lambda count: tiles(count, 2).wait_recv())
    exchange = remote(
        total_ref.at[half_of(core)], total_ref.at[half_of(core)], ssend.at[3], srecv.at[3], mate, n
    )
    exchange_from = remote(
        total_ref.at[half_of(1 - core)], total_ref.at[half_of(1 - core)], ssend.at[3], srecv.at[3],
        mate, n,
    )
    exchange.start()
    exchange_from.wait_recv()
    swap.wait_send()
    exchange.wait_send()
    for_others(lambda count: tiles(count, 1).wait_send())

    @pl.when(chip < PER_CORE)
    def _():
        remote(got_tiles, got_tiles, ssend.at[2], srecv.at[2], mate, n).wait_send()

    store_scores().wait()
    for d in range(1, 8):
        count1(d).wait_send()
    for d in range(1, groups):
        count2(d).wait_send()
    halo_geno().wait_send()
    halo_annot().wait_send()
    mate_annot().wait_send()
    for q in range(4):
        mate_geno(q).wait_send()
    for m in range(2):
        halo_back(m).wait_send()
    for q in range(4):
        where(twin_sends, q, twin(q).wait_send)


def strip_scores(dosage, annotations, table, total_variants):
    f32 = jnp.float32
    bf16 = jnp.bfloat16
    samples = dosage.shape[0]
    dma = pltpu.SemaphoreType.DMA
    hbm = pl.BlockSpec(memory_space=pltpu.HBM)
    vmem = pl.BlockSpec(memory_space=pltpu.VMEM)
    return pl.pallas_call(
        functools.partial(scores_kernel, total_variants),
        out_shape=(
            jax.ShapeDtypeStruct((128, 8 * CH), f32),
            jax.ShapeDtypeStruct((2 * PER_CORE * 8, 128), f32),
        ),
        in_specs=[hbm, hbm, hbm],
        out_specs=(hbm, vmem),
        scratch_shapes=[
            pltpu.VMEM(annotations.shape, jnp.int32),
            pltpu.VMEM((128, 8 * CH), f32),
            pltpu.VMEM((samples, 13 * CH), bf16),
            pltpu.VMEM((ROWS, 13 * CH), bf16),
            pltpu.VMEM((ROWS, 13 * CH), f32),
            pltpu.VMEM((ROWS, 4 * CH), f32),
            pltpu.VMEM((2, 5 * CH, CH), bf16),
            pltpu.VMEM((2, CH, CH), f32),
            pltpu.VMEM((2, 8, 128), f32),
            pltpu.VMEM((2, 8, 8, 128), f32),
            pltpu.VMEM((4, 128, CH), bf16),
            pltpu.VMEM((4, 128, CH), bf16),
            pltpu.VMEM((128, CH), bf16),
            pltpu.VMEM((2, 128, CH), bf16),
            pltpu.VMEM(table.shape, f32),
            pltpu.VMEM(table.shape, bf16),
            pltpu.VMEM(table.shape, bf16),
            pltpu.VMEM((2 * PER_CORE * 8, 128), f32),
            pltpu.VMEM((PER_CORE * 8, 128), f32),
            pltpu.VMEM((PER_CORE * 8, 128), f32),
            pltpu.VMEM((lax.axis_size("wide") // 2 - 1, 8, 128), f32),
            pltpu.VMEM((8, 128), f32),
            dma((11,)), dma((13,)), dma((13,)), dma((2, 8)), dma((2, 8)), dma((4,)), dma((4,)),
        ],
        compiler_params=pltpu.CompilerParams(
            collective_id=0, has_side_effects=True, vmem_limit_bytes=60 * 1024 * 1024
        ),
        name="scores",
    )(dosage, annotations, table)


def finish_kernel(total_variants, p_ref, s_hbm, ld_ref, fit_ref, s_ref, sem):
    n = lax.axis_index("narrow")
    fetch = pltpu.make_async_copy(s_hbm, s_ref, sem)
    fetch.start()
    scale = 1.0 / total_variants
    sums = p_ref[352:360, :] * scale
    m_row = sums[0:1, :]
    chi = jnp.concatenate([sums[1:2, :], sums[2:3, :]], axis=1)
    ri = lax.broadcasted_iota(jnp.int32, (128, 128), 0)
    ci = lax.broadcasted_iota(jnp.int32, (128, 128), 1)
    eye = ri == ci
    m_col = jnp.sum(jnp.where(eye, jnp.broadcast_to(m_row, (128, 128)), 0.0), axis=1, keepdims=True)
    low = ci[:64] < 64
    pair = p_ref[0:64, :]
    above = p_ref[64:96, :]
    above = jnp.concatenate([pltpu.roll(above, 64, 1), above], axis=0)
    zeros = jnp.zeros((64, 128), jnp.float32)
    above_only = jnp.concatenate([jnp.where(low, zeros, above), zeros], axis=0)
    cross = jnp.concatenate([jnp.where(low, pair, above), jnp.where(low, zeros, pair)], axis=0)
    cov = (cross + above_only.T) * scale - m_col * m_row
    proj = jnp.concatenate([p_ref[96:224, :], p_ref[224:352, :]], axis=1) * scale - m_col * chi
    var = jnp.sum(jnp.where(eye, cov, 0.0), axis=1, keepdims=True)
    rstd = 1.0 / jnp.sqrt(var + 1e-05)

    sub = lax.broadcasted_iota(jnp.int32, (8, 1), 0)

    def step(i, carry):
        a, b = carry
        cols = [jnp.broadcast_to(a[:, r : r + 1], (128, 128)) for r in range(8)]
        panel = [c[:8] for c in cols]
        right = [a[:8], b[:8, :128], b[:8, 128:]]
        for r in range(8):
            pivots = [jnp.broadcast_to(c[r : r + 1], (8, 128)) for c in panel]
            inv = 1.0 / pivots[r]
            factor = panel[r]
            here = sub == r
            for c in range(r + 1, 8):
                row = pivots[c] * inv
                panel[c] = jnp.where(here, row, panel[c] - factor * row)
            for k in range(3):
                row = jnp.broadcast_to(right[k][r : r + 1], (8, 128)) * inv
                right[k] = jnp.where(here, row, right[k] - factor * row)
        rest = [a[8:], b[8:, :128], b[8:, 128:]]
        for r in range(8):
            col = cols[r][8:]
            rest = [x - col * y[r : r + 1] for x, y in zip(rest, right)]
        a, b0, b1 = (jnp.concatenate([x, y], axis=0) for x, y in zip(rest, right))
        return pltpu.roll(a, 120, 1), jnp.concatenate([b0, b1], axis=1)

    _, coef = lax.fori_loop(0, 16, step, (cov, proj))
    fetch.wait()
    half = ld_ref.shape[1]
    own = s_ref[:, pl.ds(pl.multiple_of(n * half, half), half)]
    ld_ref[...] = (own - m_col) * rstd
    cs = split(coef)
    rows = 256
    for k in range(fit_ref.shape[0] // rows):
        dev = (s_ref[:, k * rows : (k + 1) * rows] - m_col).T
        fit_ref[k * rows : (k + 1) * rows, :] = chi + dot3(split(dev), cs, ((1,), (0,)))


def finish(totals, scores, traits, total_variants):
    return pl.pallas_call(
        functools.partial(finish_kernel, total_variants),
        out_shape=(
            jax.ShapeDtypeStruct((128, scores.shape[1] // 2), jnp.float32),
            jax.ShapeDtypeStruct((scores.shape[1], traits), jnp.float32),
        ),
        in_specs=[
            pl.BlockSpec(memory_space=pltpu.VMEM), pl.BlockSpec(memory_space=pltpu.HBM)
        ],
        out_specs=(pl.BlockSpec(memory_space=pltpu.VMEM),) * 2,
        scratch_shapes=[pltpu.VMEM(scores.shape, jnp.float32), pltpu.SemaphoreType.DMA],
        compiler_params=pltpu.CompilerParams(vmem_limit_bytes=60 * 1024 * 1024),
        name="finish",
    )(totals, scores)


def shards(dosage, annotations, test_statistic_table):
    total_variants = lax.axis_size("wide") * dosage.shape[1]
    scores, totals = strip_scores(dosage, annotations, test_statistic_table, total_variants)
    return finish(totals, scores, test_statistic_table.shape[1], total_variants)


def solution(mesh):
    in_specs = (P(None, "wide"), P(None, "wide"), P("wide", "narrow"))
    out_specs = (P(None, ("wide", "narrow")), P("wide", "narrow"))
    return jax.shard_map(shards, mesh=mesh, in_specs=in_specs, out_specs=out_specs, check_vma=False)
```

```python
import functools

import jax
import jax.numpy as jnp
from jax import lax
from jax.experimental import pallas as pl
from jax.experimental.pallas import tpu as pltpu
from jax.sharding import PartitionSpec as P

MESH = pl.DeviceIdType.MESH


def split(x):
    hi = x.astype(jnp.bfloat16)
    return hi, (x - hi.astype(jnp.float32)).astype(jnp.bfloat16)


def dot3(a, b, dims):
    ah, al = a
    bh, bl = b
    dg = functools.partial(
        lax.dot_general, dimension_numbers=(dims, ((), ())), preferred_element_type=jnp.float32
    )
    return dg(ah, bh) + (dg(ah, bl) + dg(al, bh))


CH = 256
ROWS = 144
PER_CORE = 23


def scores_kernel(
    total_variants, x_ref, ann_hbm, t_ref, out_hbm, total_ref,
    ann_ref, out_ref, geno, annot, acc, edge_acc, wbuf, edge, cnt, cnt_got, twin_out, twin_got, halo_out, halo_got,
    table, table_hi, table_lo, part, got_half, half_sum, got_tiles, tile_sum,
    load_sem, send, recv, csend, crecv, ssend, srecv,
):
    f32 = jnp.float32
    bf16 = jnp.bfloat16
    w = lax.axis_index("wide")
    n = lax.axis_index("narrow")
    wides = lax.axis_size("wide")
    samples = x_ref.shape[0]
    core = lax.rem(w, 2)
    chip = lax.div(w, 2)
    g = lax.rem(w, 8)
    h = lax.div(w, 8)
    groups = wides // 8
    chips = wides // 2
    mate = w + 1 - 2 * core
    over = lax.rem(w + 2 * core - 1 + wides, wides)
    left_chip = lax.rem(chip + core - 1 + wides // 2, wides // 2)
    turned = lax.rem(left_chip, 2)
    p = n + turned - 2 * n * turned
    csl = 2 * core + p
    base = 4 * core
    outer = 8 * core
    beside = 8 - 8 * core

    def columns(c, count=1):
        return pl.ds(pl.multiple_of(c * CH, CH), count * CH)

    def inner(i):
        return jnp.where(core == 0, 3 - i, i)

    def device(wide, narrow):
        return {"wide": wide, "narrow": narrow}

    def load(t):
        if t == 0:
            c = outer + csl
        elif t <= 4:
            c = 4 + inner(t - 1)
        else:
            c = outer + lax.rem(csl + t - 4, 4)
        return pltpu.make_async_copy(x_ref.at[:, columns(c - base)], geno.at[:, columns(c)], load_sem.at[t])

    def load_table():
        return pltpu.make_async_copy(t_ref, table, load_sem.at[8])

    def load_annotations():
        return pltpu.make_async_copy(ann_hbm, ann_ref, load_sem.at[9])

    def store_scores():
        return pltpu.make_async_copy(out_ref, out_hbm, load_sem.at[10])

    load(0).start()
    load_annotations().start()
    for t in range(1, 8):
        load(t).start()
    load_table().start()

    twin_got[...] = jnp.zeros(twin_got.shape, bf16)
    barrier = pltpu.get_barrier_semaphore()

    def hello(wide, narrow):
        pl.semaphore_signal(barrier, inc=1, device_id=device(wide, narrow), device_id_type=MESH)

    for d in range(1, 8):
        hello(w - g + lax.rem(g + d, 8), n)

    def hello_chip(d, _):
        hello(lax.rem(w + 2 * d, wides), n)
        return 0

    lax.fori_loop(1, chips, hello_chip, 0)
    hello(w, 1 - n)
    hello(over, 0)
    hello(over, 1)

    tail = jnp.where(lax.broadcasted_iota(jnp.int32, (16, CH), 0) == 0, 1.0, 0.0).astype(bf16)
    count = jnp.zeros((8, 128), f32)
    load_annotations().wait()
    for c in range(8):
        a = ann_ref[:, c * CH : (c + 1) * CH].astype(f32).astype(bf16)
        annot[0:128, columns(base + c)] = a
        annot[128:144, columns(base + c)] = tail
        count = count + lax.dot_general(
            jnp.ones((8, CH), bf16), a, (((1,), (1,)), ((), ())), preferred_element_type=f32
        )
    cnt[0] = count
    acc[...] = jnp.zeros_like(acc)
    ri = lax.broadcasted_iota(jnp.int32, (CH, CH), 0)
    ci = lax.broadcasted_iota(jnp.int32, (CH, CH), 1)
    edge[0] = jnp.where(core == 0, 0.5, jnp.where(ci <= ri, 1.0, 0.0))
    edge[1] = jnp.where(core == 1, 0.5, jnp.where(ri <= ci, 1.0, 0.0))

    def remote(src, dst, s, r, wide, narrow):
        return pltpu.make_async_remote_copy(
            src_ref=src, dst_ref=dst, send_sem=s, recv_sem=r,
            device_id=device(wide, narrow), device_id_type=MESH,
        )

    def count1(d):
        return remote(
            cnt.at[0], cnt_got.at[0, d], csend.at[0, d], crecv.at[0, d],
            w - g + lax.rem(g + d, 8), n,
        )

    def count2(d):
        return remote(
            cnt.at[1], cnt_got.at[1, d], csend.at[1, d], crecv.at[1, d],
            lax.rem(h + d, groups) * 8 + g, n,
        )

    eps = 1e-05

    def standardize(c):
        at = columns(c)
        block = 256

        def rows(i):
            return pl.ds(pl.multiple_of(i * block, block), block)

        pivot = geno[0:16, at].astype(f32)[0:1]

        def sums(i, s):
            x = (geno[rows(i), at].astype(f32) - pivot).reshape(block // 8, 8, CH)
            return s[0] + jnp.sum(x, axis=0), s[1] + jnp.sum(x * x, axis=0)

        zero = jnp.zeros((8, CH), f32)
        first, second = lax.fori_loop(0, samples // block, sums, (zero, zero))
        shift = jnp.sum(first, axis=0, keepdims=True) / samples
        var = jnp.sum(second, axis=0, keepdims=True) / samples - shift * shift
        mean = pivot + shift
        inv = 1.0 / jnp.sqrt(jnp.maximum(var, 0.0) + eps)

        def put(i, _):
            geno[rows(i), at] = ((geno[rows(i), at].astype(f32) - mean) * inv).astype(bf16)
            return 0

        lax.fori_loop(0, samples // block, put, 0)

    def halo_geno():
        return remote(
            geno.at[:, columns(outer + csl)], geno.at[:, columns(12)], send.at[0], recv.at[0], over, p
        )

    def halo_annot():
        return remote(
            annot.at[:, columns(outer + csl)], annot.at[:, columns(12)], send.at[1], recv.at[1], over, p
        )

    def mate_geno(q):
        return remote(
            geno.at[:, columns(4 + q)], geno.at[:, columns(outer + q)],
            send.at[2 + q], recv.at[2 + q], mate, n,
        )

    def mate_geno_from(q):
        return remote(
            geno.at[:, columns(4 + q)], geno.at[:, columns(beside + q)],
            send.at[2 + q], recv.at[2 + q], mate, n,
        )

    def mate_annot():
        return remote(
            annot.at[:, columns(4, 4)], annot.at[:, columns(outer, 4)], send.at[6], recv.at[6], mate, n
        )

    def mate_annot_from():
        return remote(
            annot.at[:, columns(4, 4)], annot.at[:, columns(beside, 4)], send.at[6], recv.at[6], mate, n
        )

    load(0).wait()
    standardize(outer + csl)
    pl.semaphore_wait(barrier, 7 + chips - 1 + 3)
    halo_geno().start()
    halo_annot().start()
    mate_annot().start()
    for d in range(1, 8):
        count1(d).start()
    for q in range(4):
        load(1 + q).wait()

    def mate_step(i, _):
        standardize(4 + inner(i))
        mate_geno(inner(i)).start()
        return 0

    lax.fori_loop(0, 4, mate_step, 0)
    for t in range(5, 8):
        load(t).wait()

    def rest_step(t, _):
        standardize(outer + lax.rem(csl + t, 4))
        return 0

    lax.fori_loop(1, 4, rest_step, 0)
    load_table().wait()
    table_hi[...], table_lo[...] = split(table[...])
    table_sum = jnp.sum(table[...], axis=0, keepdims=True)

    total_count = cnt[0]
    for d in range(1, 8):
        count1(d).wait_recv()
        total_count = total_count + cnt_got[0, d]
    cnt[1] = total_count
    for d in range(1, groups):
        count2(d).start()

    k1 = (1.0 + 1.0 / (samples - 2)) / (float(samples) * samples)
    k2 = 1.0 / (samples - 2)
    diff = (
        lax.broadcasted_iota(jnp.int32, (CH, CH), 0) - lax.broadcasted_iota(jnp.int32, (CH, CH), 1)
    ).astype(f32)

    def correlate(own, count, other):
        products = lax.dot_general(
            geno[:, columns(own, count)], geno[:, columns(other)], (((0,), (0,)), ((), ())),
            preferred_element_type=f32,
        )
        return (products * products) * k1 - k2

    def place(t):
        return jnp.where(core == 0, t, 7 - t), jnp.where(core == 0, t, 11 - t)

    def weigh(t):
        own, other = place(t)
        values = correlate(own, 5, other)
        for b in range(5):
            value = values[b * CH : (b + 1) * CH]
            if b in (0, 4):
                value = value * edge[b // 4]
            wbuf[lax.rem(t, 2), b * CH : (b + 1) * CH, :] = value.astype(bf16)

    def apply(t):
        own, other = place(t)
        weights = wbuf[lax.rem(t, 2)]
        acc[:, columns(other)] += jnp.dot(
            annot[:, columns(own, 5)], weights, preferred_element_type=f32
        )
        acc[:, columns(own, 5)] += lax.dot_general(
            annot[:, columns(other)], weights, (((1,), (1,)), ((), ())), preferred_element_type=f32
        )

    def step(t, _):
        apply(t - 1)
        weigh(t)
        return 0

    def inner_late(t):
        return jnp.where(core == 0, t - 4, 7 - t)

    def late_step(t, _):
        mate_geno_from(inner_late(t)).wait_recv()
        return step(t, 0)

    weigh(jnp.int32(0))
    lax.fori_loop(1, 4, step, 0)
    mate_annot_from().wait_recv()
    total_count = cnt[1]
    for d in range(1, groups):
        count2(d).wait_recv()
        total_count = total_count + cnt_got[1, d]
    apply(jnp.int32(3))
    halo_annot().wait_recv()
    halo_geno().wait_recv()
    open_end = jnp.where(core == 0, w == 0, w == wides - 1)
    near = jnp.where(open_end, 8192, jnp.where(core == 0, -8192, CH * n))
    far = jnp.where(core == 0, 512 + CH * n, 8192)
    first_row = jnp.where(core == 0, 512, 0)
    for b in range(4):
        row = ri + b * CH
        diff = row - ci
        inside = (diff >= near) & (diff <= far) & (row >= first_row)
        value = jnp.where(inside, correlate(outer + b, 1, 12), 0.0)
        wbuf[0, b * CH : (b + 1) * CH, :] = value.astype(bf16)
    weights = wbuf[0, 0 : 4 * CH, :]
    acc[:, columns(12)] = jnp.dot(
        annot[:, columns(outer, 4)], weights, preferred_element_type=f32
    )
    edge_acc[...] = lax.dot_general(
        annot[:, columns(12)], weights, (((1,), (1,)), ((), ())), preferred_element_type=f32
    )

    eye = ri[:128, :128] == ci[:128, :128]
    counts = jnp.sum(
        jnp.where(eye, jnp.broadcast_to(total_count[0:1, :], (128, 128)), 0.0),
        axis=1, keepdims=True,
    )
    shares = counts / total_variants
    zero_value = (0.0 - shares).astype(bf16).astype(f32)
    step_value = (1.0 - shares).astype(bf16).astype(f32) - zero_value

    def centred(sums):
        return zero_value * sums[128:129, :] + step_value * sums[0:128, :]

    def halo_back(m):
        return remote(
            halo_out, halo_got.at[n], send.at[7 + m], recv.at[7 + n], over, m
        )

    def halo_back_from(m):
        return remote(
            halo_out, halo_got.at[m], send.at[7 + m], recv.at[7 + m], over, m
        )

    def twin(q):
        return remote(
            twin_out.at[q], twin_got.at[q], send.at[9 + q], recv.at[9 + q], w, 1 - n
        )

    twin_sends = ((core == 1) & (n == 0), core == 1, None, (core == 1) | (n == 1))
    twin_gets = ((core == 1) & (n == 1), core == 1, None, (core == 1) | (n == 0))

    def where(conditions, q, act):
        if conditions[q] is None:
            act()
        else:
            pl.when(conditions[q])(act)

    halo_out[...] = centred(acc[:, columns(12)]).astype(bf16)
    for m in range(2):
        halo_back(m).start()
    for q in range(4):
        twin_out[q] = centred(edge_acc[:, q * CH : (q + 1) * CH]).astype(bf16)
    for q in range(4):
        where(twin_sends, q, twin(q).start)

    mate_geno_from(inner_late(4)).wait_recv()
    weigh(jnp.int32(4))
    lax.fori_loop(5, 8, late_step, 0)
    apply(jnp.int32(7))

    def out(c):
        return columns(c - base)

    for q in range(4):
        out_ref[:, out(4 + q)] = centred(acc[:, columns(4 + q)])
        out_ref[:, out(outer + q)] = centred(
            acc[:, columns(outer + q)] + edge_acc[:, q * CH : (q + 1) * CH]
        )
    for m in range(2):
        halo_back_from(m).wait_recv()
        out_ref[:, out(outer + 2 * core + m)] += halo_got[m].astype(f32)
    for q in range(4):
        where(twin_gets, q, twin(q).wait_recv)
    for q in range(4):
        out_ref[:, out(outer + q)] += twin_got[q].astype(f32)

    store_scores().start()
    dg = functools.partial(lax.dot_general, preferred_element_type=f32)
    scores = split(out_ref[...])
    proj = dot3(scores, (table_hi[...], table_lo[...]), ((1,), (0,)))
    part[96:224, :] = proj[:, :128]
    part[224:352, :] = proj[:, 128:]
    cross = dot3(scores, scores, ((1,), (1,)))
    low = lax.broadcasted_iota(jnp.int32, (64, 128), 1) < 64
    part[0:64, :] = jnp.where(low, cross[:64], cross[64:])
    part[64:96, :] = jnp.where(low[:32], pltpu.roll(cross[0:32], 64, 1), cross[32:64])
    ones = jnp.ones((8, 8 * CH), bf16)
    by_lane = (((1,), (1,)), ((), ()))
    score_sum = dg(ones, scores[0], by_lane) + dg(ones, scores[1], by_lane)
    line = lax.broadcasted_iota(jnp.int32, (8, 128), 0)
    sums = jnp.where(line == 0, score_sum, 0.0)
    sums = jnp.where(line == 1, table_sum[:, :128], sums)
    sums = jnp.where(line == 2, table_sum[:, 128:], sums)
    part[352:360, :] = sums
    part[360:368, :] = jnp.zeros((8, 128), f32)

    half_rows = PER_CORE * 8

    def tile(i):
        return pl.ds(pl.multiple_of(i * 8, 8), 8)

    def half_of(c):
        return pl.ds(pl.multiple_of(c * half_rows, 8), half_rows)

    swap = remote(part.at[half_of(1 - core)], got_half, ssend.at[0], srecv.at[0], mate, n)
    swap.start()
    swap.wait_recv()
    half_sum[...] = part[half_of(core), :] + got_half[...]

    def scatter(d, _):
        q = lax.rem(chip + d, chips)

        @pl.when(q < PER_CORE)
        def _():
            remote(
                half_sum.at[tile(q)], got_tiles.at[d - 1], ssend.at[1], srecv.at[1], 2 * q + core, n
            ).start()

        return 0

    lax.fori_loop(1, chips, scatter, 0)
    mine = core * PER_CORE + chip
    all_tiles = remote(got_tiles, got_tiles, ssend.at[1], srecv.at[1], mate, n)

    def tiles(count, i):
        ref = total_ref.at[pl.ds(0, count * 8)]
        return remote(ref, ref, ssend.at[i], srecv.at[i], mate, n)

    def for_others(act):
        pl.when(chip < PER_CORE)(lambda: act(PER_CORE - 1))
        pl.when(chip >= PER_CORE)(lambda: act(PER_CORE))

    def hand_out(d, _):
        q = lax.rem(chip + d, chips)
        remote(
            tile_sum, total_ref.at[tile(mine)], ssend.at[2], srecv.at[2], 2 * q + core, n
        ).start()
        return 0

    @pl.when(chip < PER_CORE)
    def _():
        all_tiles.wait_recv()
        total = half_sum[tile(chip), :] + jnp.sum(got_tiles[...], axis=0)
        tile_sum[...] = total
        lax.fori_loop(1, chips, hand_out, 0)
        total_ref[tile(mine), :] = total

    for_others(lambda count: tiles(count, 2).wait_recv())
    exchange = remote(
        total_ref.at[half_of(core)], total_ref.at[half_of(core)], ssend.at[3], srecv.at[3], mate, n
    )
    exchange_from = remote(
        total_ref.at[half_of(1 - core)], total_ref.at[half_of(1 - core)], ssend.at[3], srecv.at[3],
        mate, n,
    )
    exchange.start()
    exchange_from.wait_recv()
    swap.wait_send()
    exchange.wait_send()
    for_others(lambda count: tiles(count, 1).wait_send())

    @pl.when(chip < PER_CORE)
    def _():
        remote(got_tiles, got_tiles, ssend.at[2], srecv.at[2], mate, n).wait_send()

    store_scores().wait()
    for d in range(1, 8):
        count1(d).wait_send()
    for d in range(1, groups):
        count2(d).wait_send()
    halo_geno().wait_send()
    halo_annot().wait_send()
    mate_annot().wait_send()
    for q in range(4):
        mate_geno(q).wait_send()
    for m in range(2):
        halo_back(m).wait_send()
    for q in range(4):
        where(twin_sends, q, twin(q).wait_send)


def strip_scores(dosage, annotations, table, total_variants):
    f32 = jnp.float32
    bf16 = jnp.bfloat16
    samples = dosage.shape[0]
    dma = pltpu.SemaphoreType.DMA
    hbm = pl.BlockSpec(memory_space=pltpu.HBM)
    vmem = pl.BlockSpec(memory_space=pltpu.VMEM)
    return pl.pallas_call(
        functools.partial(scores_kernel, total_variants),
        out_shape=(
            jax.ShapeDtypeStruct((128, 8 * CH), f32),
            jax.ShapeDtypeStruct((2 * PER_CORE * 8, 128), f32),
        ),
        in_specs=[hbm, hbm, hbm],
        out_specs=(hbm, vmem),
        scratch_shapes=[
            pltpu.VMEM(annotations.shape, jnp.int32),
            pltpu.VMEM((128, 8 * CH), f32),
            pltpu.VMEM((samples, 13 * CH), bf16),
            pltpu.VMEM((ROWS, 13 * CH), bf16),
            pltpu.VMEM((ROWS, 13 * CH), f32),
            pltpu.VMEM((ROWS, 4 * CH), f32),
            pltpu.VMEM((2, 5 * CH, CH), bf16),
            pltpu.VMEM((2, CH, CH), f32),
            pltpu.VMEM((2, 8, 128), f32),
            pltpu.VMEM((2, 8, 8, 128), f32),
            pltpu.VMEM((4, 128, CH), bf16),
            pltpu.VMEM((4, 128, CH), bf16),
            pltpu.VMEM((128, CH), bf16),
            pltpu.VMEM((2, 128, CH), bf16),
            pltpu.VMEM(table.shape, f32),
            pltpu.VMEM(table.shape, bf16),
            pltpu.VMEM(table.shape, bf16),
            pltpu.VMEM((2 * PER_CORE * 8, 128), f32),
            pltpu.VMEM((PER_CORE * 8, 128), f32),
            pltpu.VMEM((PER_CORE * 8, 128), f32),
            pltpu.VMEM((lax.axis_size("wide") // 2 - 1, 8, 128), f32),
            pltpu.VMEM((8, 128), f32),
            dma((11,)), dma((13,)), dma((13,)), dma((2, 8)), dma((2, 8)), dma((4,)), dma((4,)),
        ],
        compiler_params=pltpu.CompilerParams(
            collective_id=0, has_side_effects=True, vmem_limit_bytes=60 * 1024 * 1024
        ),
        name="scores",
    )(dosage, annotations, table)


def finish_kernel(total_variants, p_ref, s_hbm, ld_ref, fit_ref, s_ref, sem):
    n = lax.axis_index("narrow")
    fetch = pltpu.make_async_copy(s_hbm, s_ref, sem)
    fetch.start()
    scale = 1.0 / total_variants
    sums = p_ref[352:360, :] * scale
    m_row = sums[0:1, :]
    chi = jnp.concatenate([sums[1:2, :], sums[2:3, :]], axis=1)
    ri = lax.broadcasted_iota(jnp.int32, (128, 128), 0)
    ci = lax.broadcasted_iota(jnp.int32, (128, 128), 1)
    eye = ri == ci
    m_col = jnp.sum(jnp.where(eye, jnp.broadcast_to(m_row, (128, 128)), 0.0), axis=1, keepdims=True)
    low = ci[:64] < 64
    pair = p_ref[0:64, :]
    above = p_ref[64:96, :]
    above = jnp.concatenate([pltpu.roll(above, 64, 1), above], axis=0)
    zeros = jnp.zeros((64, 128), jnp.float32)
    above_only = jnp.concatenate([jnp.where(low, zeros, above), zeros], axis=0)
    cross = jnp.concatenate([jnp.where(low, pair, above), jnp.where(low, zeros, pair)], axis=0)
    cov = (cross + above_only.T) * scale - m_col * m_row
    proj = jnp.concatenate([p_ref[96:224, :], p_ref[224:352, :]], axis=1) * scale - m_col * chi
    var = jnp.sum(jnp.where(eye, cov, 0.0), axis=1, keepdims=True)
    rstd = 1.0 / jnp.sqrt(var + 1e-05)

    sub = lax.broadcasted_iota(jnp.int32, (8, 1), 0)

    lane = lax.broadcasted_iota(jnp.int32, (8, 128), 1)
    identity = jnp.where(lane == lax.broadcasted_iota(jnp.int32, (8, 128), 0), 1.0, 0.0)
    first = lax.broadcasted_iota(jnp.int32, (120, 128), 1) < 8

    def step(i, a):
        cols = [jnp.broadcast_to(a[:, r : r + 1], (128, 128)) for r in range(8)]
        panel = [c[:8] for c in cols]
        right = jnp.where(lane < 8, identity, a[:8])
        for r in range(8):
            pivots = [jnp.broadcast_to(c[r : r + 1], (8, 128)) for c in panel]
            inv = 1.0 / pivots[r]
            factor = panel[r]
            here = sub == r
            for c in range(r + 1, 8):
                row = pivots[c] * inv
                panel[c] = jnp.where(here, row, panel[c] - factor * row)
            row = jnp.broadcast_to(right[r : r + 1], (8, 128)) * inv
            right = jnp.where(here, row, right - factor * row)
        rest = jnp.where(first, 0.0, a[8:])
        for r in range(8):
            rest = rest - cols[r][8:] * right[r : r + 1]
        return pltpu.roll(jnp.concatenate([rest, right], axis=0), 120, 1)

    inverse = lax.fori_loop(0, 16, step, cov, unroll=2)
    coef = jnp.dot(
        inverse, proj, precision=lax.Precision.HIGHEST, preferred_element_type=jnp.float32
    )
    fetch.wait()
    half = ld_ref.shape[1]
    own = s_ref[:, pl.ds(pl.multiple_of(n * half, half), half)]
    ld_ref[...] = (own - m_col) * rstd
    cs = split(coef)
    rows = 256
    for k in range(fit_ref.shape[0] // rows):
        dev = (s_ref[:, k * rows : (k + 1) * rows] - m_col).T
        fit_ref[k * rows : (k + 1) * rows, :] = chi + dot3(split(dev), cs, ((1,), (0,)))


def finish(totals, scores, traits, total_variants):
    return pl.pallas_call(
        functools.partial(finish_kernel, total_variants),
        out_shape=(
            jax.ShapeDtypeStruct((128, scores.shape[1] // 2), jnp.float32),
            jax.ShapeDtypeStruct((scores.shape[1], traits), jnp.float32),
        ),
        in_specs=[
            pl.BlockSpec(memory_space=pltpu.VMEM), pl.BlockSpec(memory_space=pltpu.HBM)
        ],
        out_specs=(pl.BlockSpec(memory_space=pltpu.VMEM),) * 2,
        scratch_shapes=[pltpu.VMEM(scores.shape, jnp.float32), pltpu.SemaphoreType.DMA],
        compiler_params=pltpu.CompilerParams(vmem_limit_bytes=60 * 1024 * 1024),
        name="finish",
    )(totals, scores)


def shards(dosage, annotations, test_statistic_table):
    total_variants = lax.axis_size("wide") * dosage.shape[1]
    scores, totals = strip_scores(dosage, annotations, test_statistic_table, total_variants)
    return finish(totals, scores, test_statistic_table.shape[1], total_variants)


def solution(mesh):
    in_specs = (P(None, "wide"), P(None, "wide"), P("wide", "narrow"))
    out_specs = (P(None, ("wide", "narrow")), P("wide", "narrow"))
    return jax.shard_map(shards, mesh=mesh, in_specs=in_specs, out_specs=out_specs, check_vma=False)
```

```python
import functools

import jax
import jax.numpy as jnp
from jax import lax
from jax.experimental import pallas as pl
from jax.experimental.pallas import tpu as pltpu
from jax.sharding import PartitionSpec as P

MESH = pl.DeviceIdType.MESH


def split(x):
    hi = x.astype(jnp.bfloat16)
    return hi, (x - hi.astype(jnp.float32)).astype(jnp.bfloat16)


def dot3(a, b, dims):
    ah, al = a
    bh, bl = b
    dg = functools.partial(
        lax.dot_general, dimension_numbers=(dims, ((), ())), preferred_element_type=jnp.float32
    )
    return dg(ah, bh) + (dg(ah, bl) + dg(al, bh))


CH = 256
ROWS = 144
PER_CORE = 23


def scores_kernel(
    total_variants, x_ref, ann_hbm, t_ref, out_hbm, total_ref,
    ann_ref, out_ref, geno, annot, acc, edge_acc, wbuf, edge, cnt, cnt_got, twin_out, twin_got, halo_out, halo_got,
    table, table_hi, table_lo, part, got_half, half_sum, got_tiles, tile_sum,
    load_sem, send, recv, csend, crecv, ssend, srecv,
):
    f32 = jnp.float32
    bf16 = jnp.bfloat16
    w = lax.axis_index("wide")
    n = lax.axis_index("narrow")
    wides = lax.axis_size("wide")
    samples = x_ref.shape[0]
    core = lax.rem(w, 2)
    chip = lax.div(w, 2)
    g = lax.rem(w, 8)
    h = lax.div(w, 8)
    groups = wides // 8
    chips = wides // 2
    mate = w + 1 - 2 * core
    over = lax.rem(w + 2 * core - 1 + wides, wides)
    left_chip = lax.rem(chip + core - 1 + wides // 2, wides // 2)
    turned = lax.rem(left_chip, 2)
    p = n + turned - 2 * n * turned
    csl = 2 * core + p
    base = 4 * core
    outer = 8 * core
    beside = 8 - 8 * core

    def columns(c, count=1):
        return pl.ds(pl.multiple_of(c * CH, CH), count * CH)

    def inner(i):
        return jnp.where(core == 0, 3 - i, i)

    def device(wide, narrow):
        return {"wide": wide, "narrow": narrow}

    def load(t):
        if t == 0:
            c = outer + csl
        elif t <= 4:
            c = 4 + inner(t - 1)
        else:
            c = outer + lax.rem(csl + t - 4, 4)
        return pltpu.make_async_copy(x_ref.at[:, columns(c - base)], geno.at[:, columns(c)], load_sem.at[t])

    def load_table():
        return pltpu.make_async_copy(t_ref, table, load_sem.at[8])

    def load_annotations():
        return pltpu.make_async_copy(ann_hbm, ann_ref, load_sem.at[9])

    def store_scores():
        return pltpu.make_async_copy(out_ref, out_hbm, load_sem.at[10])

    load(0).start()
    load_annotations().start()
    for t in range(1, 8):
        load(t).start()
    load_table().start()

    twin_got[...] = jnp.zeros(twin_got.shape, bf16)
    barrier = pltpu.get_barrier_semaphore()

    def hello(wide, narrow):
        pl.semaphore_signal(barrier, inc=1, device_id=device(wide, narrow), device_id_type=MESH)

    for d in range(1, 8):
        hello(w - g + lax.rem(g + d, 8), n)

    def hello_chip(d, _):
        hello(lax.rem(w + 2 * d, wides), n)
        return 0

    lax.fori_loop(1, chips, hello_chip, 0)
    hello(w, 1 - n)
    hello(over, 0)
    hello(over, 1)

    tail = jnp.where(lax.broadcasted_iota(jnp.int32, (16, CH), 0) == 0, 1.0, 0.0).astype(bf16)
    count = jnp.zeros((8, 128), f32)
    load_annotations().wait()
    for c in range(8):
        a = ann_ref[:, c * CH : (c + 1) * CH].astype(f32).astype(bf16)
        annot[0:128, columns(base + c)] = a
        annot[128:144, columns(base + c)] = tail
        count = count + lax.dot_general(
            jnp.ones((8, CH), bf16), a, (((1,), (1,)), ((), ())), preferred_element_type=f32
        )
    cnt[0] = count
    acc[...] = jnp.zeros_like(acc)
    ri = lax.broadcasted_iota(jnp.int32, (CH, CH), 0)
    ci = lax.broadcasted_iota(jnp.int32, (CH, CH), 1)
    edge[0] = jnp.where(core == 0, 0.5, jnp.where(ci <= ri, 1.0, 0.0))
    edge[1] = jnp.where(core == 1, 0.5, jnp.where(ri <= ci, 1.0, 0.0))

    def remote(src, dst, s, r, wide, narrow):
        return pltpu.make_async_remote_copy(
            src_ref=src, dst_ref=dst, send_sem=s, recv_sem=r,
            device_id=device(wide, narrow), device_id_type=MESH,
        )

    def count1(d):
        return remote(
            cnt.at[0], cnt_got.at[0, d], csend.at[0, d], crecv.at[0, d],
            w - g + lax.rem(g + d, 8), n,
        )

    def count2(d):
        return remote(
            cnt.at[1], cnt_got.at[1, d], csend.at[1, d], crecv.at[1, d],
            lax.rem(h + d, groups) * 8 + g, n,
        )

    eps = 1e-05

    def standardize(c):
        at = columns(c)
        block = 512

        def rows(i):
            return pl.ds(pl.multiple_of(i * block, block), block)

        pivot = geno[0:16, at].astype(f32)[0:1]

        def sums(i, s):
            x = (geno[rows(i), at].astype(f32) - pivot).reshape(block // 8, 8, CH)
            return s[0] + jnp.sum(x, axis=0), s[1] + jnp.sum(x * x, axis=0)

        zero = jnp.zeros((8, CH), f32)
        first, second = lax.fori_loop(0, samples // block, sums, (zero, zero))
        shift = jnp.sum(first, axis=0, keepdims=True) / samples
        var = jnp.sum(second, axis=0, keepdims=True) / samples - shift * shift
        mean = pivot + shift
        inv = 1.0 / jnp.sqrt(jnp.maximum(var, 0.0) + eps)

        def put(i, _):
            geno[rows(i), at] = ((geno[rows(i), at].astype(f32) - mean) * inv).astype(bf16)
            return 0

        lax.fori_loop(0, samples // block, put, 0)

    def halo_geno():
        return remote(
            geno.at[:, columns(outer + csl)], geno.at[:, columns(12)], send.at[0], recv.at[0], over, p
        )

    def halo_annot():
        return remote(
            annot.at[:, columns(outer + csl)], annot.at[:, columns(12)], send.at[1], recv.at[1], over, p
        )

    def mate_geno(q):
        return remote(
            geno.at[:, columns(4 + q)], geno.at[:, columns(outer + q)],
            send.at[2 + q], recv.at[2 + q], mate, n,
        )

    def mate_geno_from(q):
        return remote(
            geno.at[:, columns(4 + q)], geno.at[:, columns(beside + q)],
            send.at[2 + q], recv.at[2 + q], mate, n,
        )

    def mate_annot():
        return remote(
            annot.at[:, columns(4, 4)], annot.at[:, columns(outer, 4)], send.at[6], recv.at[6], mate, n
        )

    def mate_annot_from():
        return remote(
            annot.at[:, columns(4, 4)], annot.at[:, columns(beside, 4)], send.at[6], recv.at[6], mate, n
        )

    load(0).wait()
    standardize(outer + csl)
    pl.semaphore_wait(barrier, 7 + chips - 1 + 3)
    halo_geno().start()
    halo_annot().start()
    mate_annot().start()
    for d in range(1, 8):
        count1(d).start()
    for q in range(4):
        load(1 + q).wait()

    def mate_step(i, _):
        standardize(4 + inner(i))
        mate_geno(inner(i)).start()
        return 0

    lax.fori_loop(0, 4, mate_step, 0)
    for t in range(5, 8):
        load(t).wait()

    def rest_step(t, _):
        standardize(outer + lax.rem(csl + t, 4))
        return 0

    lax.fori_loop(1, 4, rest_step, 0)
    load_table().wait()
    table_hi[...], table_lo[...] = split(table[...])
    table_sum = jnp.sum(table[...], axis=0, keepdims=True)

    total_count = cnt[0]
    for d in range(1, 8):
        count1(d).wait_recv()
        total_count = total_count + cnt_got[0, d]
    cnt[1] = total_count
    for d in range(1, groups):
        count2(d).start()

    k1 = (1.0 + 1.0 / (samples - 2)) / (float(samples) * samples)
    k2 = 1.0 / (samples - 2)
    diff = (
        lax.broadcasted_iota(jnp.int32, (CH, CH), 0) - lax.broadcasted_iota(jnp.int32, (CH, CH), 1)
    ).astype(f32)

    def correlate(own, count, other):
        products = lax.dot_general(
            geno[:, columns(own, count)], geno[:, columns(other)], (((0,), (0,)), ((), ())),
            preferred_element_type=f32,
        )
        return (products * products) * k1 - k2

    def place(t):
        return jnp.where(core == 0, t, 7 - t), jnp.where(core == 0, t, 11 - t)

    def weigh(t):
        own, other = place(t)
        values = correlate(own, 5, other)
        for b in range(5):
            value = values[b * CH : (b + 1) * CH]
            if b in (0, 4):
                value = value * edge[b // 4]
            wbuf[lax.rem(t, 2), b * CH : (b + 1) * CH, :] = value.astype(bf16)

    def apply(t):
        own, other = place(t)
        weights = wbuf[lax.rem(t, 2)]
        acc[:, columns(other)] += jnp.dot(
            annot[:, columns(own, 5)], weights, preferred_element_type=f32
        )
        acc[:, columns(own, 5)] += lax.dot_general(
            annot[:, columns(other)], weights, (((1,), (1,)), ((), ())), preferred_element_type=f32
        )

    def step(t, _):
        apply(t - 1)
        weigh(t)
        return 0

    def inner_late(t):
        return jnp.where(core == 0, t - 4, 7 - t)

    def late_step(t, _):
        mate_geno_from(inner_late(t)).wait_recv()
        return step(t, 0)

    weigh(jnp.int32(0))
    lax.fori_loop(1, 4, step, 0)
    mate_annot_from().wait_recv()
    total_count = cnt[1]
    for d in range(1, groups):
        count2(d).wait_recv()
        total_count = total_count + cnt_got[1, d]
    apply(jnp.int32(3))
    halo_annot().wait_recv()
    halo_geno().wait_recv()
    open_end = jnp.where(core == 0, w == 0, w == wides - 1)
    near = jnp.where(open_end, 8192, jnp.where(core == 0, -8192, CH * n))
    far = jnp.where(core == 0, 512 + CH * n, 8192)
    first_row = jnp.where(core == 0, 512, 0)
    for b in range(4):
        row = ri + b * CH
        diff = row - ci
        inside = (diff >= near) & (diff <= far) & (row >= first_row)
        value = jnp.where(inside, correlate(outer + b, 1, 12), 0.0)
        wbuf[0, b * CH : (b + 1) * CH, :] = value.astype(bf16)
    weights = wbuf[0, 0 : 4 * CH, :]
    acc[:, columns(12)] = jnp.dot(
        annot[:, columns(outer, 4)], weights, preferred_element_type=f32
    )
    edge_acc[...] = lax.dot_general(
        annot[:, columns(12)], weights, (((1,), (1,)), ((), ())), preferred_element_type=f32
    )

    eye = ri[:128, :128] == ci[:128, :128]
    counts = jnp.sum(
        jnp.where(eye, jnp.broadcast_to(total_count[0:1, :], (128, 128)), 0.0),
        axis=1, keepdims=True,
    )
    shares = counts / total_variants
    zero_value = (0.0 - shares).astype(bf16).astype(f32)
    step_value = (1.0 - shares).astype(bf16).astype(f32) - zero_value

    def centred(sums):
        return zero_value * sums[128:129, :] + step_value * sums[0:128, :]

    def halo_back(m):
        return remote(
            halo_out, halo_got.at[n], send.at[7 + m], recv.at[7 + n], over, m
        )

    def halo_back_from(m):
        return remote(
            halo_out, halo_got.at[m], send.at[7 + m], recv.at[7 + m], over, m
        )

    def twin(q):
        return remote(
            twin_out.at[q], twin_got.at[q], send.at[9 + q], recv.at[9 + q], w, 1 - n
        )

    twin_sends = ((core == 1) & (n == 0), core == 1, None, (core == 1) | (n == 1))
    twin_gets = ((core == 1) & (n == 1), core == 1, None, (core == 1) | (n == 0))

    def where(conditions, q, act):
        if conditions[q] is None:
            act()
        else:
            pl.when(conditions[q])(act)

    halo_out[...] = centred(acc[:, columns(12)]).astype(bf16)
    for m in range(2):
        halo_back(m).start()
    for q in range(4):
        twin_out[q] = centred(edge_acc[:, q * CH : (q + 1) * CH]).astype(bf16)
    for q in range(4):
        where(twin_sends, q, twin(q).start)

    mate_geno_from(inner_late(4)).wait_recv()
    weigh(jnp.int32(4))
    lax.fori_loop(5, 8, late_step, 0)
    apply(jnp.int32(7))

    def out(c):
        return columns(c - base)

    for q in range(4):
        out_ref[:, out(4 + q)] = centred(acc[:, columns(4 + q)])
        out_ref[:, out(outer + q)] = centred(
            acc[:, columns(outer + q)] + edge_acc[:, q * CH : (q + 1) * CH]
        )
    for m in range(2):
        halo_back_from(m).wait_recv()
        out_ref[:, out(outer + 2 * core + m)] += halo_got[m].astype(f32)
    for q in range(4):
        where(twin_gets, q, twin(q).wait_recv)
    for q in range(4):
        out_ref[:, out(outer + q)] += twin_got[q].astype(f32)

    store_scores().start()
    dg = functools.partial(lax.dot_general, preferred_element_type=f32)
    scores = split(out_ref[...])
    proj = dot3(scores, (table_hi[...], table_lo[...]), ((1,), (0,)))
    part[96:224, :] = proj[:, :128]
    part[224:352, :] = proj[:, 128:]
    cross = dot3(scores, scores, ((1,), (1,)))
    low = lax.broadcasted_iota(jnp.int32, (64, 128), 1) < 64
    part[0:64, :] = jnp.where(low, cross[:64], cross[64:])
    part[64:96, :] = jnp.where(low[:32], pltpu.roll(cross[0:32], 64, 1), cross[32:64])
    ones = jnp.ones((8, 8 * CH), bf16)
    by_lane = (((1,), (1,)), ((), ()))
    score_sum = dg(ones, scores[0], by_lane) + dg(ones, scores[1], by_lane)
    line = lax.broadcasted_iota(jnp.int32, (8, 128), 0)
    sums = jnp.where(line == 0, score_sum, 0.0)
    sums = jnp.where(line == 1, table_sum[:, :128], sums)
    sums = jnp.where(line == 2, table_sum[:, 128:], sums)
    part[352:360, :] = sums
    part[360:368, :] = jnp.zeros((8, 128), f32)

    half_rows = PER_CORE * 8

    def tile(i):
        return pl.ds(pl.multiple_of(i * 8, 8), 8)

    def half_of(c):
        return pl.ds(pl.multiple_of(c * half_rows, 8), half_rows)

    swap = remote(part.at[half_of(1 - core)], got_half, ssend.at[0], srecv.at[0], mate, n)
    swap.start()
    swap.wait_recv()
    half_sum[...] = part[half_of(core), :] + got_half[...]

    def scatter(d, _):
        q = lax.rem(chip + d, chips)

        @pl.when(q < PER_CORE)
        def _():
            remote(
                half_sum.at[tile(q)], got_tiles.at[d - 1], ssend.at[1], srecv.at[1], 2 * q + core, n
            ).start()

        return 0

    lax.fori_loop(1, chips, scatter, 0)
    mine = core * PER_CORE + chip
    all_tiles = remote(got_tiles, got_tiles, ssend.at[1], srecv.at[1], mate, n)

    def tiles(count, i):
        ref = total_ref.at[pl.ds(0, count * 8)]
        return remote(ref, ref, ssend.at[i], srecv.at[i], mate, n)

    def for_others(act):
        pl.when(chip < PER_CORE)(lambda: act(PER_CORE - 1))
        pl.when(chip >= PER_CORE)(lambda: act(PER_CORE))

    def hand_out(d, _):
        q = lax.rem(chip + d, chips)
        remote(
            tile_sum, total_ref.at[tile(mine)], ssend.at[2], srecv.at[2], 2 * q + core, n
        ).start()
        return 0

    @pl.when(chip < PER_CORE)
    def _():
        all_tiles.wait_recv()
        total = half_sum[tile(chip), :] + jnp.sum(got_tiles[...], axis=0)
        tile_sum[...] = total
        lax.fori_loop(1, chips, hand_out, 0)
        total_ref[tile(mine), :] = total

    for_others(lambda count: tiles(count, 2).wait_recv())
    exchange = remote(
        total_ref.at[half_of(core)], total_ref.at[half_of(core)], ssend.at[3], srecv.at[3], mate, n
    )
    exchange_from = remote(
        total_ref.at[half_of(1 - core)], total_ref.at[half_of(1 - core)], ssend.at[3], srecv.at[3],
        mate, n,
    )
    exchange.start()
    exchange_from.wait_recv()
    swap.wait_send()
    exchange.wait_send()
    for_others(lambda count: tiles(count, 1).wait_send())

    @pl.when(chip < PER_CORE)
    def _():
        remote(got_tiles, got_tiles, ssend.at[2], srecv.at[2], mate, n).wait_send()

    store_scores().wait()
    for d in range(1, 8):
        count1(d).wait_send()
    for d in range(1, groups):
        count2(d).wait_send()
    halo_geno().wait_send()
    halo_annot().wait_send()
    mate_annot().wait_send()
    for q in range(4):
        mate_geno(q).wait_send()
    for m in range(2):
        halo_back(m).wait_send()
    for q in range(4):
        where(twin_sends, q, twin(q).wait_send)


def strip_scores(dosage, annotations, table, total_variants):
    f32 = jnp.float32
    bf16 = jnp.bfloat16
    samples = dosage.shape[0]
    dma = pltpu.SemaphoreType.DMA
    hbm = pl.BlockSpec(memory_space=pltpu.HBM)
    vmem = pl.BlockSpec(memory_space=pltpu.VMEM)
    return pl.pallas_call(
        functools.partial(scores_kernel, total_variants),
        out_shape=(
            jax.ShapeDtypeStruct((128, 8 * CH), f32),
            jax.ShapeDtypeStruct((2 * PER_CORE * 8, 128), f32),
        ),
        in_specs=[hbm, hbm, hbm],
        out_specs=(hbm, vmem),
        scratch_shapes=[
            pltpu.VMEM(annotations.shape, jnp.int32),
            pltpu.VMEM((128, 8 * CH), f32),
            pltpu.VMEM((samples, 13 * CH), bf16),
            pltpu.VMEM((ROWS, 13 * CH), bf16),
            pltpu.VMEM((ROWS, 13 * CH), f32),
            pltpu.VMEM((ROWS, 4 * CH), f32),
            pltpu.VMEM((2, 5 * CH, CH), bf16),
            pltpu.VMEM((2, CH, CH), f32),
            pltpu.VMEM((2, 8, 128), f32),
            pltpu.VMEM((2, 8, 8, 128), f32),
            pltpu.VMEM((4, 128, CH), bf16),
            pltpu.VMEM((4, 128, CH), bf16),
            pltpu.VMEM((128, CH), bf16),
            pltpu.VMEM((2, 128, CH), bf16),
            pltpu.VMEM(table.shape, f32),
            pltpu.VMEM(table.shape, bf16),
            pltpu.VMEM(table.shape, bf16),
            pltpu.VMEM((2 * PER_CORE * 8, 128), f32),
            pltpu.VMEM((PER_CORE * 8, 128), f32),
            pltpu.VMEM((PER_CORE * 8, 128), f32),
            pltpu.VMEM((lax.axis_size("wide") // 2 - 1, 8, 128), f32),
            pltpu.VMEM((8, 128), f32),
            dma((11,)), dma((13,)), dma((13,)), dma((2, 8)), dma((2, 8)), dma((4,)), dma((4,)),
        ],
        compiler_params=pltpu.CompilerParams(
            collective_id=0, has_side_effects=True, vmem_limit_bytes=60 * 1024 * 1024
        ),
        name="scores",
    )(dosage, annotations, table)


def finish_kernel(total_variants, p_ref, s_hbm, ld_ref, fit_ref, s_ref, sem):
    n = lax.axis_index("narrow")
    fetch = pltpu.make_async_copy(s_hbm, s_ref, sem)
    fetch.start()
    scale = 1.0 / total_variants
    sums = p_ref[352:360, :] * scale
    m_row = sums[0:1, :]
    chi = jnp.concatenate([sums[1:2, :], sums[2:3, :]], axis=1)
    ri = lax.broadcasted_iota(jnp.int32, (128, 128), 0)
    ci = lax.broadcasted_iota(jnp.int32, (128, 128), 1)
    eye = ri == ci
    m_col = jnp.sum(jnp.where(eye, jnp.broadcast_to(m_row, (128, 128)), 0.0), axis=1, keepdims=True)
    low = ci[:64] < 64
    pair = p_ref[0:64, :]
    above = p_ref[64:96, :]
    above = jnp.concatenate([pltpu.roll(above, 64, 1), above], axis=0)
    zeros = jnp.zeros((64, 128), jnp.float32)
    above_only = jnp.concatenate([jnp.where(low, zeros, above), zeros], axis=0)
    cross = jnp.concatenate([jnp.where(low, pair, above), jnp.where(low, zeros, pair)], axis=0)
    cov = (cross + above_only.T) * scale - m_col * m_row
    proj = jnp.concatenate([p_ref[96:224, :], p_ref[224:352, :]], axis=1) * scale - m_col * chi
    var = jnp.sum(jnp.where(eye, cov, 0.0), axis=1, keepdims=True)
    rstd = 1.0 / jnp.sqrt(var + 1e-05)

    sub = lax.broadcasted_iota(jnp.int32, (8, 1), 0)

    lane = lax.broadcasted_iota(jnp.int32, (8, 128), 1)
    identity = jnp.where(lane == lax.broadcasted_iota(jnp.int32, (8, 128), 0), 1.0, 0.0)
    first = lax.broadcasted_iota(jnp.int32, (120, 128), 1) < 8

    def step(i, a):
        cols = [jnp.broadcast_to(a[:, r : r + 1], (128, 128)) for r in range(8)]
        panel = [c[:8] for c in cols]
        right = jnp.where(lane < 8, identity, a[:8])
        for r in range(8):
            pivots = [jnp.broadcast_to(c[r : r + 1], (8, 128)) for c in panel]
            inv = 1.0 / pivots[r]
            factor = panel[r]
            here = sub == r
            for c in range(r + 1, 8):
                row = pivots[c] * inv
                panel[c] = jnp.where(here, row, panel[c] - factor * row)
            row = jnp.broadcast_to(right[r : r + 1], (8, 128)) * inv
            right = jnp.where(here, row, right - factor * row)
        rest = jnp.where(first, 0.0, a[8:])
        for r in range(8):
            rest = rest - cols[r][8:] * right[r : r + 1]
        return pltpu.roll(jnp.concatenate([rest, right], axis=0), 120, 1)

    inverse = lax.fori_loop(0, 16, step, cov, unroll=2)
    coef = jnp.dot(
        inverse, proj, precision=lax.Precision.HIGHEST, preferred_element_type=jnp.float32
    )
    fetch.wait()
    half = ld_ref.shape[1]
    own = s_ref[:, pl.ds(pl.multiple_of(n * half, half), half)]
    ld_ref[...] = (own - m_col) * rstd
    cs = split(coef)
    rows = 256
    for k in range(fit_ref.shape[0] // rows):
        dev = (s_ref[:, k * rows : (k + 1) * rows] - m_col).T
        fit_ref[k * rows : (k + 1) * rows, :] = chi + dot3(split(dev), cs, ((1,), (0,)))


def finish(totals, scores, traits, total_variants):
    return pl.pallas_call(
        functools.partial(finish_kernel, total_variants),
        out_shape=(
            jax.ShapeDtypeStruct((128, scores.shape[1] // 2), jnp.float32),
            jax.ShapeDtypeStruct((scores.shape[1], traits), jnp.float32),
        ),
        in_specs=[
            pl.BlockSpec(memory_space=pltpu.VMEM), pl.BlockSpec(memory_space=pltpu.HBM)
        ],
        out_specs=(pl.BlockSpec(memory_space=pltpu.VMEM),) * 2,
        scratch_shapes=[pltpu.VMEM(scores.shape, jnp.float32), pltpu.SemaphoreType.DMA],
        compiler_params=pltpu.CompilerParams(vmem_limit_bytes=60 * 1024 * 1024),
        name="finish",
    )(totals, scores)


def shards(dosage, annotations, test_statistic_table):
    total_variants = lax.axis_size("wide") * dosage.shape[1]
    scores, totals = strip_scores(dosage, annotations, test_statistic_table, total_variants)
    return finish(totals, scores, test_statistic_table.shape[1], total_variants)


def solution(mesh):
    in_specs = (P(None, "wide"), P(None, "wide"), P("wide", "narrow"))
    out_specs = (P(None, ("wide", "narrow")), P("wide", "narrow"))
    return jax.shard_map(shards, mesh=mesh, in_specs=in_specs, out_specs=out_specs, check_vma=False)
```
